512 devices in a mesh: row: 32 (over x, y, core), col: 16 (over z).
Axes of the slice: x: 4, y: 4, z: 16, core: 2. Of those that a mesh axis runs over, the one named last changes fastest.
Arguments:
- amplitudes: float32 [4096, 2, 256], P(('row', 'col')), may hold values from -18 to 18
- integrals: float32 [2, 256, 102400], P(None, 'row', 'col'), may hold values from -0.25 to 0.25
- occ_pairs: int32 [4096, 2], P('row'), may hold values from 0 to 199
- eps_occ: float32 [200], replicated, may hold values from -2 to -0.5
- eps_vir: float32 [800], replicated, may hold values from 0.2 to 3
- vir_offset: int32 [1], replicated, may hold values from 0 to 672
Outputs:
- update: float32 [4096, 102400], P('row', 'col')
The draws below stay inside these ranges and needn't reach their ends.
All inputs are finite; a program needn't handle non-finite values.
Results may differ from the reference program's by a relative error of at most 0.00007.
Values sent between devices are 32-bit elements; how exact they have to be, the bound alone decides.
A program may use at most 64 MiB of HBM per device.

```python
import jax
import jax.numpy as jnp
from jax import lax

NO = 200
NV = 800
A_BLK = 128
PANEL = 256
STEPS = 2
IJ = 4096
AB = 102400


def touch_ends(values, stream_key, least, largest):
    spot = [jax.random.randint(jax.random.fold_in(stream_key, axis), (), 0, length) for axis, length in enumerate(values.shape)]
    widest = values.shape.index(max(values.shape))
    next_to = spot[:widest] + [(spot[widest] + 1) % values.shape[widest]] + spot[widest + 1:]
    return values.at[tuple(spot)].set(least).at[tuple(next_to)].set(largest)


def block_scale(stream_key, extent, split, smallest, top_value):
    def one(dim, shards_of):
        draws = jax.random.uniform(jax.random.fold_in(jax.random.fold_in(stream_key, 6), dim), (shards_of,), jnp.float32, smallest / len(split), top_value / len(split))
        return jnp.repeat(jnp.exp(draws), extent[dim] // shards_of).reshape((-1,) + (1,) * (len(extent) - dim - 1))

    loudness = one(*split[0])
    for cut in split[1:]:
        loudness = loudness * one(*cut)
    return loudness


def noise(stream_key, dims, deviation, limit, split=(), dtype=jnp.bfloat16):
    entries = jax.random.normal(stream_key, dims, jnp.float32) * deviation
    if len(split) > 0:
        entries = block_scale(stream_key, dims, split, -0.22, 0.18) * entries
    return jnp.clip(entries, min=-limit, max=limit).astype(dtype)


def setup_inputs(seed: int = 0) -> dict:
    streams_of = jax.random.split(jax.random.key(seed), 7)
    amplitudes = noise(streams_of[0], (IJ, STEPS, PANEL), 3.0, 18.0, ((0, 512),), jnp.float32)
    integrals = noise(streams_of[1], (STEPS, PANEL, AB), (STEPS * PANEL) ** -0.5, 0.25, ((1, 32), (2, 16)), jnp.float32)
    occ_pairs = touch_ends(jax.random.randint(streams_of[2], (IJ, 2), 0, NO), jax.random.fold_in(streams_of[2], 1), 0, NO - 1).astype(jnp.int32)
    eps_occ = jnp.clip(jax.random.uniform(streams_of[3], (NO,), jnp.float32, -2.0, -0.5), -2.0, -0.5)
    eps_vir = jnp.clip(jax.random.uniform(streams_of[4], (NV,), jnp.float32, 0.2, 3.0), 0.2, 3.0)
    vir_offset = jax.random.randint(streams_of[5], (1,), 0, NV - A_BLK + 1).astype(jnp.int32)
    return dict(amplitudes=amplitudes, integrals=integrals, occ_pairs=occ_pairs, eps_occ=eps_occ, eps_vir=eps_vir, vir_offset=vir_offset)


def reference(amplitudes, integrals, occ_pairs, eps_occ, eps_vir, vir_offset):
    flat_amp = amplitudes.reshape(IJ, STEPS * PANEL)
    flat_int = integrals.reshape(STEPS * PANEL, A_BLK * NV)
    ladder = jnp.dot(flat_amp, flat_int, preferred_element_type=jnp.float32, precision=lax.Precision.HIGHEST)
    pair_energy = eps_occ[occ_pairs[:, 0]] + eps_occ[occ_pairs[:, 1]]
    block_energy = lax.dynamic_slice(eps_vir, (vir_offset[0].astype(jnp.int32),), (A_BLK,))
    vir_energy = (block_energy[:, None] + eps_vir[None, :]).reshape(-1)
    return ladder / (pair_energy[:, None] - vir_energy[None, :])
```

```python
import functools

import jax
import jax.numpy as jnp
from jax import lax
from jax.experimental import pallas as pl
from jax.experimental.pallas import tpu as pltpu
from jax.sharding import PartitionSpec as P

MESH = pl.DeviceIdType.MESH
SIDE = 4
DEPTH = 16
WIDTH = 640
AHEAD = 3


def gather_kernel(
    amp_ref, int_ref, occ_ref, eocc_ref, evir_ref, off_ref, out_ref,
    rows, amps, both, pair, vir,
    send, recv, zsend, zrecv, own,
):
    row, z = lax.axis_index("row"), lax.axis_index("col")
    x, y, core = row // 8, (row // 2) % SIDE, row % 2
    way = 1 - 2 * core
    width = WIDTH
    parts = int_ref.shape[2] // width

    def at(xx, yy, cc):
        return {"row": (xx * SIDE + yy) * 2 + cc, "col": z}

    def along(panel, first, step):
        to = (lambda v: (v + step + SIDE) % SIDE)
        if (panel == 0) == first:
            return at(to(x), y, core)
        return at(x, to(y), core)

    sibling = at(x, y, 1 - core)
    peers = [along(0, True, 1), along(0, True, -1), along(0, False, 1), along(0, False, -1), sibling]
    peers += [{"row": row, "col": (z + j) % DEPTH} for j in range(1, DEPTH)]
    barrier = pltpu.get_barrier_semaphore()
    for peer in peers:
        pl.semaphore_signal(barrier, inc=1, device_id=peer, device_id_type=MESH)
    pl.semaphore_wait(barrier, len(peers))

    def cols(k):
        return pl.ds(k * width, width)

    def copy(kind, panel, k, src, dst, to):
        return pltpu.make_async_remote_copy(
            src_ref=src, dst_ref=dst, send_sem=send.at[kind, panel, k], recv_sem=recv.at[kind, panel, k],
            device_id=to, device_id_type=MESH,
        )

    def one(panel, k, back):
        if panel == 0:
            return rows.at[0, (x - back + SIDE) % SIDE, y, core, :, cols(k)]
        return rows.at[1, x, (y - back + SIDE) % SIDE, core, :, cols(k)]

    def line(panel, k, back):
        if panel == 0:
            return rows.at[0, :, (y - back + SIDE) % SIDE, core, :, cols(k)]
        return rows.at[1, (x - back + SIDE) % SIDE, :, core, :, cols(k)]

    def ahead(p, k):
        return copy(0, p, k, int_ref.at[p, :, cols(k)], one(p, k, 0), along(p, True, way))

    def behind(p, k):
        return copy(1, p, k, int_ref.at[p, :, cols(k)], one(p, k, 0), along(p, True, -way))

    def onward(p, k):
        src = one(p, k, way)
        return copy(2, p, k, src, src, along(p, True, way))

    def line_ahead(p, k):
        src = line(p, k, 0)
        return copy(3, p, k, src, src, along(p, False, way))

    def line_behind(p, k):
        src = line(p, k, 0)
        return copy(4, p, k, src, src, along(p, False, -way))

    def line_onward(p, k):
        src = line(p, k, way)
        return copy(5, p, k, src, src, along(p, False, way))

    def across(p, k):
        src = rows.at[p, :, :, core, :, cols(k)]
        return copy(6, p, k, src, src, sibling)

    both_panels = (0, 1)
    own_copy = pltpu.make_async_copy(int_ref, rows.at[:, x, y, core], own.at[0])
    own_copy.start()
    amp_copy = pltpu.make_async_copy(amp_ref, amps.at[z], own.at[1])
    amp_copy.start()

    def start_own(k):
        for p in both_panels:
            ahead(p, k).start()
            behind(p, k).start()

    start_own(0)

    def amp_send(j):
        return pltpu.make_async_remote_copy(
            src_ref=amp_ref, dst_ref=amps.at[z], send_sem=zsend.at[j], recv_sem=zrecv.at[j],
            device_id={"row": row, "col": (z + j) % DEPTH}, device_id_type=MESH,
        )

    for k in range(1, AHEAD):
        start_own(k)
    for j in range(1, DEPTH):
        amp_send(j).start()

    lanes = lax.broadcasted_iota(jnp.int32, (occ_ref.shape[0], eocc_ref.shape[1]), 1)
    energy = eocc_ref[...]
    occ_sum = jnp.sum(jnp.where(lanes == occ_ref[:, 0:1], energy, 0.0), axis=1, keepdims=True)
    occ_sum = occ_sum + jnp.sum(jnp.where(lanes == occ_ref[:, 1:2], energy, 0.0), axis=1, keepdims=True)
    pair[...] = jnp.broadcast_to(occ_sum, pair.shape)
    virtual = evir_ref[...]
    spots = lax.broadcasted_iota(jnp.int32, virtual.shape, 1)
    count = int_ref.shape[2] // virtual.shape[1]
    first = off_ref[0] + z * count
    vir[...] = jnp.concatenate(
        [jnp.sum(jnp.where(spots == first + a, virtual, 0.0), axis=1, keepdims=True) + virtual for a in range(count)],
        axis=1,
    )

    def split_amps():
        amp_copy.wait()
        for j in range(1, DEPTH):
            amp_send(j).wait()
        high_low = amps[...].reshape(both.shape[0] // 2, both.shape[1])
        high = high_low.astype(jnp.bfloat16)
        both[: high.shape[0], :] = high
        both[high.shape[0] :, :] = (high_low - high.astype(jnp.float32)).astype(jnp.bfloat16)

    def compute(k):
        n = out_ref.shape[0]
        block = rows[:, :, :, :, :, cols(k)].reshape(both.shape[1], width)
        high = block.astype(jnp.bfloat16)
        low = (block - high.astype(jnp.float32)).astype(jnp.bfloat16)
        head = jnp.dot(both[...], high, preferred_element_type=jnp.float32)
        tail = jnp.dot(both[:n, :], low, preferred_element_type=jnp.float32)
        ladder = head[:n] + (head[n:] + tail)
        energy = pair[:, 0:1] - vir[:, cols(k)]
        out_ref[:, cols(k)] = ladder / energy

    for t in range(parts + 5):
        if AHEAD <= t + AHEAD < parts:
            start_own(t + AHEAD)
        if t < parts:
            for p in both_panels:
                ahead(p, t).wait_recv()
                onward(p, t).start()
        k = t - 1
        if 0 <= k < parts:
            if k == 0:
                own_copy.wait()
            for p in both_panels:
                behind(p, k).wait_recv()
                onward(p, k).wait_recv()
                line_ahead(p, k).start()
                line_behind(p, k).start()
        k = t - 3
        if 0 <= k < parts:
            for p in both_panels:
                line_ahead(p, k).wait_recv()
                line_onward(p, k).start()
        k = t - 4
        if 0 <= k < parts:
            for p in both_panels:
                line_behind(p, k).wait_recv()
                line_onward(p, k).wait_recv()
                across(p, k).start()
        k = t - 5
        if 0 <= k < parts:
            if k == 0:
                split_amps()
            for p in both_panels:
                across(p, k).wait_recv()
            compute(k)

    for k in range(parts):
        for p in both_panels:
            for made in (ahead, behind, onward, line_ahead, line_behind, line_onward, across):
                made(p, k).wait_send()


def store_kernel(src_ref, dst_ref, sems):
    count = sems.shape[0]
    height = src_ref.shape[0] // count
    copies = [
        pltpu.make_async_copy(src_ref.at[pl.ds(i * height, height)], dst_ref.at[pl.ds(i * height, height)], sems.at[i])
        for i in range(count)
    ]
    for one in copies:
        one.start()
    for one in copies:
        one.wait()


def shards(amplitudes, integrals, occ_pairs, eps_occ, eps_vir, vir_offset):
    panels, depth, ab = integrals.shape
    mine, _, panel = amplitudes.shape
    pairs = occ_pairs.shape[0]
    cd = panels * panel
    parts = ab // WIDTH
    vmem = pl.BlockSpec(memory_space=pltpu.VMEM)
    update = pl.pallas_call(
        gather_kernel,
        out_shape=pltpu.VMEM((pairs, ab), jnp.float32),
        in_specs=[vmem, pl.BlockSpec(memory_space=pl.ANY), vmem, vmem, vmem, pl.BlockSpec(memory_space=pltpu.SMEM)],
        out_specs=vmem,
        scratch_shapes=[
            pltpu.VMEM((panels, SIDE, SIDE, 2, depth, ab), jnp.float32),
            pltpu.VMEM((DEPTH, mine, cd), jnp.float32),
            pltpu.VMEM((2 * pairs, cd), jnp.bfloat16),
            pltpu.VMEM((pairs, 128), jnp.float32),
            pltpu.VMEM((1, ab), jnp.float32),
            pltpu.SemaphoreType.DMA((7, 2, parts)),
            pltpu.SemaphoreType.DMA((7, 2, parts)),
            pltpu.SemaphoreType.DMA((DEPTH,)),
            pltpu.SemaphoreType.DMA((DEPTH,)),
            pltpu.SemaphoreType.DMA((2,)),
        ],
        compiler_params=pltpu.CompilerParams(
            collective_id=0, has_side_effects=True, vmem_limit_bytes=40 * 1024 * 1024
        ),
        cost_estimate=pl.CostEstimate(
            flops=2 * pairs * cd * ab * 3, bytes_accessed=4 * (pairs * ab + panels * depth * ab), transcendentals=0
        ),
        name="gather_and_contract",
    )(
        amplitudes.reshape(mine, cd),
        integrals,
        occ_pairs,
        eps_occ.reshape(1, -1),
        eps_vir.reshape(1, -1),
        vir_offset,
    )
    return pl.pallas_call(
        store_kernel,
        out_shape=jax.ShapeDtypeStruct((pairs, ab), jnp.float32),
        in_specs=[vmem],
        out_specs=pl.BlockSpec(memory_space=pl.ANY),
        scratch_shapes=[pltpu.SemaphoreType.DMA((8,))],
        cost_estimate=pl.CostEstimate(flops=0, bytes_accessed=4 * pairs * ab, transcendentals=0),
        name="store",
    )(pltpu.with_memory_space_constraint(update, pltpu.VMEM))


def solution(mesh):
    return jax.shard_map(
        shards,
        mesh=mesh,
        in_specs=(
            P(("row", "col"), None, None),
            P(None, "row", "col"),
            P("row", None),
            P(),
            P(),
            P(),
        ),
        out_specs=P("row", "col"),
        check_vma=False,
    )
```

```python
import functools

import jax
import jax.numpy as jnp
from jax import lax
from jax.experimental import pallas as pl
from jax.experimental.pallas import tpu as pltpu
from jax.sharding import PartitionSpec as P

MESH = pl.DeviceIdType.MESH
SIDE = 4
DEPTH = 16
PIECES = (640, 2560)
PARTS = (640, 768, 768, 640, 384)


def gather_kernel(
    amp_hbm, int_hbm, occ_hbm, eocc_hbm, evir_hbm, off_ref, out_ref,
    rows, slabs, amps, both, pair, vir, stage,
    amp_ref, occ_ref, eocc_ref, evir_ref,
    local, send, near, far, ring, side,
):
    row, z = lax.axis_index("row"), lax.axis_index("col")
    x, y, core = row // 8, (row // 2) % SIDE, row % 2
    way = 1 - 2 * core
    half = int_hbm.shape[2] // 2
    mine = pl.multiple_of(core * half, 128)
    pairs = out_ref.shape[0]
    panels = (0, 1)

    def shift(v, step, size=SIDE):
        return (v + step + size) % size

    def at(xx, yy, cc):
        return {"row": (xx * SIDE + yy) * 2 + cc, "col": z}

    def along(panel, phase, step, cc):
        if panel == phase:
            return at(shift(x, step), y, cc)
        return at(x, shift(y, step), cc)

    sibling = at(x, y, 1 - core)

    def fetch(i, src, dst):
        return pltpu.make_async_copy(src, dst, local.at[i])

    fetches = [
        fetch(0, int_hbm.at[:, :, pl.ds(mine, half)], rows.at[:, x, y, core]),
        fetch(1, amp_hbm, amp_ref),
        fetch(2, occ_hbm, occ_ref),
        fetch(3, eocc_hbm, eocc_ref),
        fetch(4, evir_hbm, evir_ref),
    ]
    for one in fetches:
        one.start()

    peers = [along(0, phase, step, cc) for phase in (0, 1) for step in (1, -1) for cc in (0, 1)]
    peers += [sibling] + [{"row": row, "col": shift(z, step, DEPTH)} for step in (1, -1)]
    barrier = pltpu.get_barrier_semaphore()
    for peer in peers:
        pl.semaphore_signal(barrier, inc=1, device_id=peer, device_id_type=MESH)
    pl.semaphore_wait(barrier, len(peers))

    def remote(src, dst, sent, got, to):
        return pltpu.make_async_remote_copy(
            src_ref=src, dst_ref=dst, send_sem=sent, recv_sem=got, device_id=to, device_id_type=MESH
        )

    starts = [sum(PIECES[:a]) for a in range(len(PIECES))]

    def chip(p, a, back):
        cols = pl.ds(starts[a], PIECES[a])
        if p == 0:
            return rows.at[0, shift(x, -back), y, :, :, cols]
        return rows.at[1, x, shift(y, -back), :, :, cols]

    def first_direct(p, a, step, cc):
        src = int_hbm.at[p, :, pl.ds(cc * half + starts[a], PIECES[a])]
        dst = rows.at[p, x, y, core, :, pl.ds(starts[a], PIECES[a])]
        return remote(src, dst, send.at[0], near.at[(1 - step) // 2, p, a], along(p, 0, step, cc))

    def first(p, a, step):
        return remote(chip(p, a, 0), chip(p, a, 0), send.at[0], near.at[(1 - step) // 2, p, a], along(p, 0, step, core))

    def first_arrived(p, a, index):
        remote(chip(p, a, 0), chip(p, a, 0), send.at[0], near.at[index, p, a], sibling).wait_recv()

    def first_onward(p, a):
        return remote(chip(p, a, way), chip(p, a, way), send.at[0], near.at[2, p, a], along(p, 0, way, core))

    begins = [sum(PARTS[:k]) for k in range(len(PARTS))]

    def line(p, k, back):
        cols = pl.ds(begins[k], PARTS[k])
        if p == 0:
            return rows.at[0, :, shift(y, -back), :, :, cols]
        return rows.at[1, shift(x, -back), :, :, :, cols]

    def second(p, k, kind):
        back, step = ((0, way), (0, -way), (way, way))[kind]
        return remote(line(p, k, back), line(p, k, back), send.at[1], far.at[kind, p, k], along(p, 1, step, core))

    steps = DEPTH // 2
    base = core * steps

    def ring_copy(s):
        src = slabs.at[0] if s == 1 else slabs.at[base + s - 1]
        return remote(src, slabs.at[base + s], send.at[2], ring.at[s - 1], {"row": row, "col": shift(z, way, DEPTH)})

    halves = remote(
        int_hbm.at[:, :, pl.ds(pl.multiple_of((1 - core) * half, 128), half)],
        rows.at[:, x, y, core], send.at[3], side.at[0], sibling,
    )
    own_slab = remote(slabs.at[0, core], slabs.at[0, core], send.at[4], side.at[1], sibling)
    pair_copy = remote(pair.at[core], pair.at[core], send.at[5], side.at[2], sibling)
    share = remote(slabs.at[pl.ds(base + 1, steps)], slabs.at[pl.ds(base + 1, steps)], send.at[6], side.at[3], sibling)

    def result(k):
        cols = pl.ds(begins[k], PARTS[k])
        there = out_ref.at[:, pl.ds(pl.multiple_of(mine + begins[k], 128), PARTS[k])]
        return remote(stage.at[:, cols], there, send.at[7], side.at[4], sibling)

    halves.start()
    for p in panels:
        for step in (1, -1):
            for cc in (0, 1):
                first_direct(p, 0, step, cc).start()

    fetches[1].wait()
    width = amp_ref.shape[2]
    for p in panels:
        slabs[0, core, :, p * width : (p + 1) * width] = amp_ref[:, p, :]
    own_slab.start()
    fetches[0].wait()
    halves.wait_recv()
    for a in range(1, len(PIECES)):
        for p in panels:
            for step in (1, -1):
                first(p, a, step).start()
    for p in panels:
        first_arrived(p, 0, core)
        first_onward(p, 0).start()
    own_slab.wait_recv()
    ring_copy(1).start()

    for one in fetches[2:]:
        one.wait()
    occ_count = eocc_ref.shape[0]
    levels = jnp.broadcast_to(eocc_ref[...].reshape(1, occ_count), (pairs, occ_count)).T
    spots = lax.broadcasted_iota(jnp.int32, levels.shape, 0)
    energy = [jnp.sum(jnp.where(spots == occ_ref[i : i + 1, :], levels, 0.0), axis=0, keepdims=True) for i in (0, 1)]
    pair[core] = jnp.broadcast_to(energy[0] + energy[1], (pairs, pairs)).T
    pair_copy.start()
    virtual = evir_ref[...].reshape(1, evir_ref.shape[0])
    spots = lax.broadcasted_iota(jnp.int32, virtual.shape, 1)
    count = half // virtual.shape[1]
    lead = off_ref[0] + (2 * z + core) * count
    vir[...] = jnp.concatenate(
        [jnp.sum(jnp.where(spots == lead + a, virtual, 0.0), axis=1, keepdims=True) + virtual for a in range(count)],
        axis=1,
    )

    def ring_step(s):
        if s > steps:
            return
        ring_copy(s).wait_recv()
        if s < steps:
            ring_copy(s + 1).start()
        else:
            share.start()

    def split_amps():
        share.wait_recv()
        pair_copy.wait_recv()
        for j in range(DEPTH):
            back = -j if j <= steps else j - steps
            amps[shift(z, back, DEPTH)] = slabs[j]
        for i, c in enumerate((core, 1 - core)):
            full = amps[:, c].reshape(pairs, amps.shape[3])
            high = full.astype(jnp.bfloat16)
            both[i * pairs : (i + 1) * pairs, :] = high
            both[(2 + i) * pairs : (3 + i) * pairs, :] = (full - high.astype(jnp.float32)).astype(jnp.bfloat16)

    def compute(k):
        cols = pl.ds(begins[k], PARTS[k])
        block = rows[:, :, :, :, :, cols].reshape(both.shape[1], PARTS[k])
        high = block.astype(jnp.bfloat16)
        low = (block - high.astype(jnp.float32)).astype(jnp.bfloat16)
        head = jnp.dot(both[...], high, preferred_element_type=jnp.float32)
        tail = jnp.dot(both[: 2 * pairs, :], low, preferred_element_type=jnp.float32)
        ladder = head[: 2 * pairs] + (head[2 * pairs :] + tail)
        stage[:, cols] = ladder[pairs:] / (pair[1 - core][:, 0:1] - vir[:, cols])
        result(k).start()
        there = pl.ds(pl.multiple_of(mine + begins[k], 128), PARTS[k])
        out_ref[:, there] = ladder[:pairs] / (pair[core][:, 0:1] - vir[:, cols])

    def start_second(k):
        for p in panels:
            second(p, k, 0).start()
            second(p, k, 1).start()

    def onward_second(k):
        for p in panels:
            second(p, k, 0).wait_recv()
            second(p, k, 2).start()

    def finish(k):
        for p in panels:
            second(p, k, 1).wait_recv()
            second(p, k, 2).wait_recv()
        compute(k)

    for p in panels:
        first_arrived(p, 0, 1 - core)
        first_arrived(p, 0, 2)
    start_second(0)
    for a in range(1, len(PIECES)):
        for p in panels:
            first_arrived(p, a, core)
            first_onward(p, a).start()
    ring_step(1)
    for a in range(1, len(PIECES)):
        for p in panels:
            first_arrived(p, a, 1 - core)
            first_arrived(p, a, 2)
    count = len(PARTS)
    done = 2
    for k in range(1, count + 1):
        if k < count:
            start_second(k)
        if k == 1:
            ring_step(done)
            done += 1
        onward_second(k - 1)
        for _ in range(2):
            ring_step(done)
            done += 1
        if k == count - 1:
            while done <= steps:
                ring_step(done)
                done += 1
            split_amps()
            for j in range(count - 2):
                finish(j)
    finish(count - 2)
    finish(count - 1)

    remote(rows.at[0, 0:3, 0:2], rows.at[0, 0:3, 0:2], send.at[0], side.at[0], sibling).wait_send()
    remote(rows.at[:, :, 0:3], rows.at[:, :, 0:3], send.at[1], side.at[0], sibling).wait_send()
    remote(slabs.at[pl.ds(0, steps)], slabs.at[pl.ds(0, steps)], send.at[2], side.at[0], sibling).wait_send()
    for one in (halves, own_slab, pair_copy, share):
        one.wait_send()
    all_results = remote(stage, out_ref.at[:, pl.ds(mine, half)], send.at[7], side.at[4], sibling)
    all_results.wait_send()
    all_results.wait_recv()


def store_kernel(src_ref, dst_ref, sems):
    count = sems.shape[0]
    height = src_ref.shape[0] // count
    copies = [
        pltpu.make_async_copy(src_ref.at[pl.ds(i * height, height)], dst_ref.at[pl.ds(i * height, height)], sems.at[i])
        for i in range(count)
    ]
    for one in copies:
        one.start()
    for one in copies:
        one.wait()


def gather_and_contract(amplitudes, integrals, occ_pairs, eps_occ, eps_vir, vir_offset, cid=0, name="gather_and_contract"):
    panels, depth, ab = integrals.shape
    mine, _, panel = amplitudes.shape
    pairs = occ_pairs.shape[0]
    cd = panels * panel
    half = ab // 2
    hbm = pl.BlockSpec(memory_space=pltpu.HBM)
    arrays = (amplitudes, integrals, occ_pairs.T, eps_occ, eps_vir)
    return pl.pallas_call(
        gather_kernel,
        out_shape=pltpu.VMEM((pairs, ab), jnp.float32),
        in_specs=[hbm] * 5 + [pl.BlockSpec(memory_space=pltpu.SMEM)],
        out_specs=pl.BlockSpec(memory_space=pltpu.VMEM),
        scratch_shapes=[
            pltpu.VMEM((panels, SIDE, SIDE, 2, depth, half), jnp.float32),
            pltpu.VMEM((DEPTH + 1, 2, mine, cd), jnp.float32),
            pltpu.VMEM((DEPTH, 2, mine, cd), jnp.float32),
            pltpu.VMEM((4 * pairs, cd), jnp.bfloat16),
            pltpu.VMEM((2, pairs, pairs), jnp.float32),
            pltpu.VMEM((1, half), jnp.float32),
            pltpu.VMEM((pairs, half), jnp.float32),
            pltpu.VMEM(amplitudes.shape, jnp.float32),
            pltpu.VMEM((2, pairs), jnp.int32),
            pltpu.VMEM(eps_occ.shape, jnp.float32),
            pltpu.VMEM(eps_vir.shape, jnp.float32),
            pltpu.SemaphoreType.DMA((5,)),
            pltpu.SemaphoreType.DMA((8,)),
            pltpu.SemaphoreType.DMA((3, 2, len(PIECES))),
            pltpu.SemaphoreType.DMA((3, 2, len(PARTS))),
            pltpu.SemaphoreType.DMA((DEPTH // 2,)),
            pltpu.SemaphoreType.DMA((5,)),
        ],
        compiler_params=pltpu.CompilerParams(
            collective_id=cid, has_side_effects=True, vmem_limit_bytes=40 * 1024 * 1024
        ),
        cost_estimate=pl.CostEstimate(
            flops=2 * pairs * cd * ab * 3, bytes_accessed=4 * (pairs * ab + panels * depth * ab), transcendentals=0
        ),
        name=name,
    )(*(pltpu.with_memory_space_constraint(a, pltpu.HBM) for a in arrays), vir_offset)


def shards(amplitudes, integrals, occ_pairs, eps_occ, eps_vir, vir_offset):
    update = gather_and_contract(amplitudes, integrals, occ_pairs, eps_occ, eps_vir, vir_offset)
    return pl.pallas_call(
        store_kernel,
        out_shape=jax.ShapeDtypeStruct(update.shape, jnp.float32),
        in_specs=[pl.BlockSpec(memory_space=pltpu.VMEM)],
        out_specs=pl.BlockSpec(memory_space=pl.ANY),
        scratch_shapes=[pltpu.SemaphoreType.DMA((8,))],
        cost_estimate=pl.CostEstimate(flops=0, bytes_accessed=4 * update.size, transcendentals=0),
        name="store",
    )(pltpu.with_memory_space_constraint(update, pltpu.VMEM))


def solution(mesh):
    return jax.shard_map(
        shards,
        mesh=mesh,
        in_specs=(
            P(("row", "col"), None, None),
            P(None, "row", "col"),
            P("row", None),
            P(),
            P(),
            P(),
        ),
        out_specs=P("row", "col"),
        check_vma=False,
    )
```

```python
import functools

import jax
import jax.numpy as jnp
from jax import lax
from jax.experimental import pallas as pl
from jax.experimental.pallas import tpu as pltpu
from jax.sharding import PartitionSpec as P

MESH = pl.DeviceIdType.MESH
SIDE = 4
DEPTH = 16
REACH = 3
PIECES = (640, 2560)
PARTS = (640, 768, 768, 640, 384)


def gather_kernel(
    amp_hbm, int_hbm, occ_hbm, eocc_hbm, evir_hbm, off_ref, out_ref,
    rows, slabs, amps, both, pair, vir, stage,
    amp_ref, occ_ref, eocc_ref, evir_ref,
    local, send, near, onto, far, over, line_send, line_got, side,
):
    row, z = lax.axis_index("row"), lax.axis_index("col")
    x, y, core = row // 8, (row // 2) % SIDE, row % 2
    way = 1 - 2 * core
    half = int_hbm.shape[2] // 2
    mine = pl.multiple_of(core * half, 128)
    pairs = out_ref.shape[0]
    panels = (0, 1)

    def turn(v):
        return (v + SIDE) % SIDE

    def beside(axis, step, cc):
        if axis == 0:
            return {"row": (turn(x + step) * SIDE + y) * 2 + cc, "col": z}
        return {"row": (x * SIDE + turn(y + step)) * 2 + cc, "col": z}

    sibling = {"row": row + way, "col": z}

    def there(d):
        return jnp.logical_and(z + d >= 0, z + d < DEPTH)

    def fetch(i, src, dst):
        return pltpu.make_async_copy(src, dst, local.at[i])

    fetches = [
        fetch(0, int_hbm.at[:, :, pl.ds(mine, half)], rows.at[:, 0, 0, core]),
        fetch(1, amp_hbm, amp_ref),
        fetch(2, occ_hbm, occ_ref),
        fetch(3, eocc_hbm, eocc_ref),
        fetch(4, evir_hbm, evir_ref),
    ]
    for one in fetches:
        one.start()

    barrier = pltpu.get_barrier_semaphore()

    def greet(to):
        pl.semaphore_signal(barrier, inc=1, device_id=to, device_id_type=MESH)

    greeted = 9
    greet(sibling)
    for axis in (0, 1):
        for step in (1, -1):
            for cc in (0, 1):
                greet(beside(axis, step, cc))
    for d in range(1, REACH + 1):
        for dd in (d, -d):
            pl.when(there(dd))(functools.partial(greet, {"row": row, "col": z + dd}))
            greeted = greeted + there(dd).astype(jnp.int32)
    pl.semaphore_wait(barrier, greeted)

    def remote(src, dst, sent, got, to):
        return pltpu.make_async_remote_copy(
            src_ref=src, dst_ref=dst, send_sem=sent, recv_sem=got, device_id=to, device_id_type=MESH
        )

    starts = [sum(PIECES[:a]) for a in range(len(PIECES))]
    begins = [sum(PARTS[:k]) for k in range(len(PARTS))]

    def place(p, along_first, along_second, cols):
        if p == 0:
            return rows.at[0, along_first, along_second, :, :, cols]
        return rows.at[1, along_second, along_first, :, :, cols]

    def own_direct(axis, step, cc):
        src = int_hbm.at[:, :, pl.ds(pl.multiple_of(cc * half, 128), PIECES[0])]
        back = (-step) % SIDE
        spot = (slice(None), back, 0) if axis == 0 else (slice(None), 0, back)
        dst = rows.at[(*spot, core, slice(None), pl.ds(0, PIECES[0]))]
        return remote(src, dst, send.at[0], near.at[0, axis, 0, (1 - step) // 2], beside(axis, step, cc))

    def own_direct_arrived(axis, index):
        block = rows.at[:, 0, 0, :, :, pl.ds(0, PIECES[0])]
        remote(block, block, send.at[0], near.at[0, axis, 0, index], sibling).wait_recv()

    def own(a, p, phase, step):
        cols = pl.ds(starts[a], PIECES[a])
        back = (-step) % SIDE
        dst = place(p, back, 0, cols) if phase == 0 else place(p, 0, back, cols)
        axis = phase if p == 0 else 1 - phase
        return remote(place(p, 0, 0, cols), dst, send.at[0], near.at[a, p, phase, (1 - step) // 2], beside(axis, step, core))

    def own_arrived(a, p, phase, index):
        block = place(p, 0, 0, pl.ds(starts[a], PIECES[a]))
        remote(block, block, send.at[0], near.at[a, p, phase, index], sibling).wait_recv()

    def onward(a, p):
        cols = pl.ds(starts[a], PIECES[a])
        return remote(place(p, turn(-way), 0, cols), place(p, 2, 0, cols), send.at[0], onto.at[a, p], beside(p, way, core))

    def others(k, p, step):
        cols = pl.ds(begins[k], PARTS[k])
        three = pl.ds(1, SIDE - 1)
        return remote(
            place(p, three, 0, cols), place(p, three, (-step) % SIDE, cols),
            send.at[0], far.at[k, p, (1 - step) // 2], beside(1 - p, step, core),
        )

    def others_arrived(k, p, index):
        block = place(p, pl.ds(1, SIDE - 1), 0, pl.ds(begins[k], PARTS[k]))
        remote(block, block, send.at[0], far.at[k, p, index], sibling).wait_recv()

    def line_onward(k, p):
        cols = pl.ds(begins[k], PARTS[k])
        whole = pl.ds(0, SIDE)
        return remote(place(p, whole, turn(-way), cols), place(p, whole, 2, cols), send.at[0], over.at[k, p], beside(1 - p, way, core))

    zero = DEPTH - 1
    blocks = zero // REACH

    def slab_block(s):
        low = zero - REACH * s if s > 0 else zero
        return slabs.at[pl.ds(low + core * (2 * (zero - low) - REACH + 1), REACH)]

    def slab_copy(d):
        return remote(slabs.at[zero], slabs.at[zero - way * d], line_send.at[d - 1], line_got.at[d - 1], {"row": row, "col": z + way * d})

    def block_copy(s):
        i = REACH + s - 1
        return remote(slab_block(s), slab_block(s + 1), line_send.at[i], line_got.at[i], {"row": row, "col": z + way * REACH})

    def line_step(s):
        if s == 0:
            own_slab.wait_recv()
            for d in range(1, REACH + 1):
                pl.when(there(way * d))(slab_copy(d).start)
            return
        if s == 1:
            for d in range(1, REACH + 1):
                pl.when(there(-way * d))(slab_copy(d).wait_recv)
        else:
            pl.when(there(-way * REACH))(block_copy(s - 1).wait_recv)
        if s < blocks:
            pl.when(there(way * REACH))(block_copy(s).start)
        else:
            share.start()

    halves = remote(
        int_hbm.at[:, :, pl.ds(pl.multiple_of((1 - core) * half, 128), half)],
        rows.at[:, 0, 0, core], send.at[1], side.at[0], sibling,
    )
    own_slab = remote(slabs.at[zero, core], slabs.at[zero, core], send.at[2], side.at[1], sibling)
    pair_copy = remote(pair.at[core], pair.at[core], send.at[3], side.at[2], sibling)
    side_slabs = slabs.at[pl.ds(core * DEPTH, zero)]
    share = remote(side_slabs, side_slabs, send.at[4], side.at[3], sibling)

    def result(k):
        block = out_ref.at[:, pl.ds(pl.multiple_of(mine + begins[k], 128), PARTS[k])]
        return remote(stage.at[:, pl.ds(begins[k], PARTS[k])], block, send.at[5], side.at[4], sibling)

    def denominators():
        for one in fetches[2:]:
            one.wait()
        occ_count = eocc_ref.shape[0]
        levels = jnp.broadcast_to(eocc_ref[...].reshape(1, occ_count), (pairs, occ_count)).T
        spots = lax.broadcasted_iota(jnp.int32, levels.shape, 0)
        energy = [jnp.sum(jnp.where(spots == occ_ref[i : i + 1, :], levels, 0.0), axis=0, keepdims=True) for i in (0, 1)]
        pair[core] = jnp.broadcast_to(energy[0] + energy[1], (pairs, pairs)).T
        pair_copy.start()
        virtual = evir_ref[...].reshape(1, evir_ref.shape[0])
        spots = lax.broadcasted_iota(jnp.int32, virtual.shape, 1)
        count = half // virtual.shape[1]
        lead = off_ref[0] + (2 * z + core) * count
        vir[...] = jnp.concatenate(
            [jnp.sum(jnp.where(spots == lead + a, virtual, 0.0), axis=1, keepdims=True) + virtual for a in range(count)],
            axis=1,
        )

    def split_amps():
        share.wait_recv()
        pair_copy.wait_recv()
        for a in range(DEPTH):
            amps[a] = slabs[zero + a - z]
        for i, c in enumerate((core, 1 - core)):
            full = amps[:, c].reshape(pairs, amps.shape[3])
            high = full.astype(jnp.bfloat16)
            both[i * pairs : (i + 1) * pairs, :] = high
            both[(2 + i) * pairs : (3 + i) * pairs, :] = (full - high.astype(jnp.float32)).astype(jnp.bfloat16)

    def compute(k):
        cols = pl.ds(begins[k], PARTS[k])
        block = jnp.concatenate(
            [rows[p, turn(i - x), turn(j - y), :, :, cols].reshape(-1, PARTS[k]) for p in panels for i in range(SIDE) for j in range(SIDE)],
            axis=0,
        )
        high = block.astype(jnp.bfloat16)
        low = (block - high.astype(jnp.float32)).astype(jnp.bfloat16)
        head = jnp.dot(both[...], high, preferred_element_type=jnp.float32)
        tail = jnp.dot(both[: 2 * pairs, :], low, preferred_element_type=jnp.float32)
        ladder = head[: 2 * pairs] + (head[2 * pairs :] + tail)
        stage[:, cols] = ladder[pairs:] / (pair[1 - core][:, 0:1] - vir[:, cols])
        result(k).start()
        spot = pl.ds(pl.multiple_of(mine + begins[k], 128), PARTS[k])
        out_ref[:, spot] = ladder[:pairs] / (pair[core][:, 0:1] - vir[:, cols])

    def send_others(k):
        for p in panels:
            for step in (1, -1):
                others(k, p, step).start()

    def send_line_onward(k):
        if k == 1:
            for p in panels:
                own_arrived(1, p, 1, core)
        for p in panels:
            others_arrived(k, p, core)
            line_onward(k, p).start()

    def finish(k):
        if k == 1:
            for p in panels:
                own_arrived(1, p, 1, 1 - core)
        for p in panels:
            others_arrived(k, p, 1 - core)
            line_onward(k, p).wait_recv()
        compute(k)

    halves.start()
    for axis in (0, 1):
        for step in (1, -1):
            for cc in (0, 1):
                own_direct(axis, step, cc).start()
    fetches[1].wait()
    width = amp_ref.shape[2]
    for p in panels:
        slabs[zero, core, :, p * width : (p + 1) * width] = amp_ref[:, p, :]
    own_slab.start()
    fetches[0].wait()
    halves.wait_recv()
    for p in panels:
        for step in (1, -1):
            own(1, p, 0, step).start()
    for axis in (0, 1):
        own_direct_arrived(axis, core)
    for p in panels:
        onward(0, p).start()
    for p in panels:
        for step in (1, -1):
            own(1, p, 1, step).start()
    line_step(0)
    denominators()
    for axis in (0, 1):
        own_direct_arrived(axis, 1 - core)
    for p in panels:
        onward(0, p).wait_recv()
    send_others(0)
    line_step(1)
    for p in panels:
        own_arrived(1, p, 0, core)
        onward(1, p).start()
    line_step(2)
    for p in panels:
        own_arrived(1, p, 0, 1 - core)
        onward(1, p).wait_recv()
    send_others(1)
    count = len(PARTS)
    for k in range(count):
        send_line_onward(k)
        if k + 2 < count:
            send_others(k + 2)
        if k + 3 <= blocks:
            line_step(k + 3)
            if k + 3 == blocks:
                split_amps()
        if k >= 2:
            finish(k - 2)
    finish(count - 2)
    finish(count - 1)

    for block in (rows.at[:, :, 0:3], rows.at[0, 0:3, 0:2]):
        remote(block, block, send.at[0], side.at[0], sibling).wait_send()
    for one in (halves, own_slab, pair_copy, share):
        one.wait_send()
    for d in range(1, REACH + 1):
        pl.when(there(way * d))(slab_copy(d).wait_send)
    for s in range(1, blocks):
        pl.when(there(way * REACH))(block_copy(s).wait_send)
    all_results = remote(stage, out_ref.at[:, pl.ds(mine, half)], send.at[5], side.at[4], sibling)
    all_results.wait_send()
    all_results.wait_recv()


def store_kernel(src_ref, dst_ref, sems):
    count = sems.shape[0]
    height = src_ref.shape[0] // count
    copies = [
        pltpu.make_async_copy(src_ref.at[pl.ds(i * height, height)], dst_ref.at[pl.ds(i * height, height)], sems.at[i])
        for i in range(count)
    ]
    for one in copies:
        one.start()
    for one in copies:
        one.wait()


def gather_and_contract(amplitudes, integrals, occ_pairs, eps_occ, eps_vir, vir_offset, cid=0, name="gather_and_contract"):
    panels, depth, ab = integrals.shape
    mine, _, panel = amplitudes.shape
    pairs = occ_pairs.shape[0]
    cd = panels * panel
    half = ab // 2
    hbm = pl.BlockSpec(memory_space=pltpu.HBM)
    arrays = (amplitudes, integrals, occ_pairs.T, eps_occ, eps_vir)
    return pl.pallas_call(
        gather_kernel,
        out_shape=pltpu.VMEM((pairs, ab), jnp.float32),
        in_specs=[hbm] * 5 + [pl.BlockSpec(memory_space=pltpu.SMEM)],
        out_specs=pl.BlockSpec(memory_space=pltpu.VMEM),
        scratch_shapes=[
            pltpu.VMEM((panels, SIDE, SIDE, 2, depth, half), jnp.float32),
            pltpu.VMEM((2 * DEPTH - 1, 2, mine, cd), jnp.float32),
            pltpu.VMEM((DEPTH, 2, mine, cd), jnp.float32),
            pltpu.VMEM((4 * pairs, cd), jnp.bfloat16),
            pltpu.VMEM((2, pairs, pairs), jnp.float32),
            pltpu.VMEM((1, half), jnp.float32),
            pltpu.VMEM((pairs, half), jnp.float32),
            pltpu.VMEM(amplitudes.shape, jnp.float32),
            pltpu.VMEM((2, pairs), jnp.int32),
            pltpu.VMEM(eps_occ.shape, jnp.float32),
            pltpu.VMEM(eps_vir.shape, jnp.float32),
            pltpu.SemaphoreType.DMA((5,)),
            pltpu.SemaphoreType.DMA((6,)),
            pltpu.SemaphoreType.DMA((len(PIECES), 2, 2, 2)),
            pltpu.SemaphoreType.DMA((len(PIECES), 2)),
            pltpu.SemaphoreType.DMA((len(PARTS), 2, 2)),
            pltpu.SemaphoreType.DMA((len(PARTS), 2)),
            pltpu.SemaphoreType.DMA((2 * REACH + 1,)),
            pltpu.SemaphoreType.DMA((2 * REACH + 1,)),
            pltpu.SemaphoreType.DMA((5,)),
        ],
        compiler_params=pltpu.CompilerParams(
            collective_id=cid, has_side_effects=True, vmem_limit_bytes=40 * 1024 * 1024
        ),
        cost_estimate=pl.CostEstimate(
            flops=2 * pairs * cd * ab * 3, bytes_accessed=4 * (pairs * ab + panels * depth * ab), transcendentals=0
        ),
        name=name,
    )(*(pltpu.with_memory_space_constraint(a, pltpu.HBM) for a in arrays), vir_offset)


def shards(amplitudes, integrals, occ_pairs, eps_occ, eps_vir, vir_offset):
    update = gather_and_contract(amplitudes, integrals, occ_pairs, eps_occ, eps_vir, vir_offset)
    return pl.pallas_call(
        store_kernel,
        out_shape=jax.ShapeDtypeStruct(update.shape, jnp.float32),
        in_specs=[pl.BlockSpec(memory_space=pltpu.VMEM)],
        out_specs=pl.BlockSpec(memory_space=pl.ANY),
        scratch_shapes=[pltpu.SemaphoreType.DMA((8,))],
        cost_estimate=pl.CostEstimate(flops=0, bytes_accessed=4 * update.size, transcendentals=0),
        name="store",
    )(pltpu.with_memory_space_constraint(update, pltpu.VMEM))


def solution(mesh):
    return jax.shard_map(
        shards,
        mesh=mesh,
        in_specs=(
            P(("row", "col"), None, None),
            P(None, "row", "col"),
            P("row", None),
            P(),
            P(),
            P(),
        ),
        out_specs=P("row", "col"),
        check_vma=False,
    )
```

```python
import functools

import jax
import jax.numpy as jnp
from jax import lax
from jax.experimental import pallas as pl
from jax.experimental.pallas import tpu as pltpu
from jax.sharding import PartitionSpec as P

MESH = pl.DeviceIdType.MESH
SIDE = 4
DEPTH = 16
REACH = 3
LAST = 4
PIECES = (640, 2560)
PARTS = (640, 768, 768, 640, 384)
POINTS = (0, 1, 2, 3, 4)


def gather_kernel(
    amp_hbm, int_hbm, occ_hbm, eocc_hbm, evir_hbm, off_ref, out_ref,
    rows, slabs, amps, both, pair, vir, stage,
    amp_ref, occ_ref, eocc_ref, evir_ref,
    local, send, near, onto, far, over, line_send, line_got, side, ready,
):
    row, z = lax.axis_index("row"), lax.axis_index("col")
    x, y, core = row // 8, (row // 2) % SIDE, row % 2
    way = 1 - 2 * core
    half = int_hbm.shape[2] // 2
    mine = pl.multiple_of(core * half, 128)
    pairs = out_ref.shape[0]
    panels = (0, 1)

    def turn(v):
        return (v + SIDE) % SIDE

    def beside(axis, step, cc):
        if axis == 0:
            return {"row": (turn(x + step) * SIDE + y) * 2 + cc, "col": z}
        return {"row": (x * SIDE + turn(y + step)) * 2 + cc, "col": z}

    sibling = {"row": row + way, "col": z}

    zero = DEPTH - 1
    blocks = zero // REACH

    def down_blocks(v):
        return jnp.where(v + 2 * REACH <= zero, 2, 1)

    def blocks_at(v):
        return jnp.where(core == 0, blocks - down_blocks(v), down_blocks(v))

    def on_line(d):
        return {"row": row, "col": (z + d + DEPTH) % DEPTH}

    def target(d):
        return z + way * d

    def sends(d, count):
        inside = jnp.logical_or(core == 0, target(d) >= 0)
        return jnp.logical_and(inside, blocks_at((target(d) + DEPTH) % DEPTH) >= count)

    def sends_slab(d):
        return sends(d, 1)

    def gets_slab(d):
        return jnp.logical_or(core == 0, z + d <= zero)

    def seam_to(d):
        return jnp.logical_and(core == 1, z < d)

    def seam_from(d):
        return jnp.logical_and(core == 1, z + d > zero)

    def sends_block(s):
        return sends(REACH, s + 1)

    def gets_block(s):
        return blocks_at(z) >= s + 1

    def fetch(i, src, dst):
        return pltpu.make_async_copy(src, dst, local.at[i])

    fetches = [
        fetch(0, int_hbm.at[:, :, pl.ds(mine, half)], rows.at[:, 0, 0, core]),
        fetch(1, amp_hbm, amp_ref),
        fetch(2, occ_hbm, occ_ref),
        fetch(3, eocc_hbm, eocc_ref),
        fetch(4, evir_hbm, evir_ref),
    ]
    for one in fetches:
        one.start()

    barrier = pltpu.get_barrier_semaphore()

    def greet(to):
        pl.semaphore_signal(barrier, inc=1, device_id=to, device_id_type=MESH)

    greeted = 9
    greet(sibling)
    for axis in (0, 1):
        for step in (1, -1):
            for cc in (0, 1):
                greet(beside(axis, step, cc))
    for d in range(1, REACH + 1):
        pl.when(gets_slab(d))(functools.partial(greet, on_line(-way * d)))
        pl.when(seam_to(d))(functools.partial(greet, on_line(way * d)))
        greeted = greeted + sends_slab(d).astype(jnp.int32) + seam_from(d).astype(jnp.int32)
    pl.semaphore_wait(barrier, greeted)

    def tell(to):
        pl.semaphore_signal(ready, inc=1, device_id=to, device_id_type=MESH)

    for d in range(1, REACH + 1):
        pl.when(seam_from(d))(functools.partial(tell, on_line(-way * d)))

    def remote(src, dst, sent, got, to):
        return pltpu.make_async_remote_copy(
            src_ref=src, dst_ref=dst, send_sem=sent, recv_sem=got, device_id=to, device_id_type=MESH
        )

    starts = [sum(PIECES[:a]) for a in range(len(PIECES))]
    begins = [sum(PARTS[:k]) for k in range(len(PARTS))]

    def place(p, along_first, along_second, cols):
        if p == 0:
            return rows.at[0, along_first, along_second, :, :, cols]
        return rows.at[1, along_second, along_first, :, :, cols]

    def own_direct(axis, step, cc):
        src = int_hbm.at[:, :, pl.ds(pl.multiple_of(cc * half, 128), PIECES[0])]
        back = (-step) % SIDE
        spot = (slice(None), back, 0) if axis == 0 else (slice(None), 0, back)
        dst = rows.at[(*spot, core, slice(None), pl.ds(0, PIECES[0]))]
        return remote(src, dst, send.at[0], near.at[0, axis, 0, (1 - step) // 2], beside(axis, step, cc))

    def own_direct_arrived(axis, index):
        block = rows.at[:, 0, 0, :, :, pl.ds(0, PIECES[0])]
        remote(block, block, send.at[0], near.at[0, axis, 0, index], sibling).wait_recv()

    def own(a, p, phase, step):
        cols = pl.ds(starts[a], PIECES[a])
        back = (-step) % SIDE
        dst = place(p, back, 0, cols) if phase == 0 else place(p, 0, back, cols)
        axis = phase if p == 0 else 1 - phase
        return remote(place(p, 0, 0, cols), dst, send.at[0], near.at[a, p, phase, (1 - step) // 2], beside(axis, step, core))

    def own_arrived(a, p, phase, index):
        block = place(p, 0, 0, pl.ds(starts[a], PIECES[a]))
        remote(block, block, send.at[0], near.at[a, p, phase, index], sibling).wait_recv()

    def onward(a, p):
        cols = pl.ds(starts[a], PIECES[a])
        return remote(place(p, turn(-way), 0, cols), place(p, 2, 0, cols), send.at[0], onto.at[a, p], beside(p, way, core))

    def others(k, p, step):
        cols = pl.ds(begins[k], PARTS[k])
        three = pl.ds(1, SIDE - 1)
        return remote(
            place(p, three, 0, cols), place(p, three, (-step) % SIDE, cols),
            send.at[0], far.at[k, p, (1 - step) // 2], beside(1 - p, step, core),
        )

    def others_arrived(k, p, index):
        block = place(p, pl.ds(1, SIDE - 1), 0, pl.ds(begins[k], PARTS[k]))
        remote(block, block, send.at[0], far.at[k, p, index], sibling).wait_recv()

    def line_onward(k, p):
        cols = pl.ds(begins[k], PARTS[k])
        whole = pl.ds(0, SIDE)
        return remote(place(p, whole, turn(-way), cols), place(p, whole, 2, cols), send.at[0], over.at[k, p], beside(1 - p, way, core))

    def slab_block(s):
        low = zero - REACH * s if s > 0 else zero
        return slabs.at[pl.ds(low + core * (2 * (zero - low) - REACH + 1), REACH)]

    def slab_copy(d):
        return remote(slabs.at[zero], slabs.at[zero - way * d], line_send.at[d - 1], line_got.at[d - 1], on_line(way * d))

    def block_copy(s):
        i = REACH + s - 1
        return remote(slab_block(s), slab_block(s + 1), line_send.at[i], line_got.at[i], on_line(way * REACH))

    def line_step(s):
        if s == 0:
            own_slab.wait_recv()
            for d in range(1, REACH + 1):
                pl.when(sends_slab(d))(slab_copy(d).start)
            return
        if s == 1:
            for d in range(1, REACH + 1):
                pl.when(gets_slab(d))(slab_copy(d).wait_recv)
        else:
            pl.when(gets_block(s - 1))(block_copy(s - 1).wait_recv)
        if s == 2:
            late = sum(seam_to(d).astype(jnp.int32) for d in range(1, REACH + 1))
            pl.when(late > 0)(functools.partial(pl.semaphore_wait, ready, late))
            for d in range(1, REACH + 1):
                pl.when(seam_to(d))(slab_copy(d).start)
        if s < LAST:
            pl.when(sends_block(s))(block_copy(s).start)
        else:
            for d in range(1, REACH + 1):
                pl.when(seam_from(d))(slab_copy(d).wait_recv)
            share.start()

    halves = remote(
        int_hbm.at[:, :, pl.ds(pl.multiple_of((1 - core) * half, 128), half)],
        rows.at[:, 0, 0, core], send.at[1], side.at[0], sibling,
    )
    own_slab = remote(slabs.at[zero, core], slabs.at[zero, core], send.at[2], side.at[1], sibling)
    pair_copy = remote(pair.at[core], pair.at[core], send.at[3], side.at[2], sibling)
    side_slabs = slabs.at[pl.ds(core * DEPTH, zero)]
    share = remote(side_slabs, side_slabs, send.at[4], side.at[3], sibling)

    def result(k):
        block = out_ref.at[:, pl.ds(pl.multiple_of(mine + begins[k], 128), PARTS[k])]
        return remote(stage.at[:, pl.ds(begins[k], PARTS[k])], block, send.at[5], side.at[4], sibling)

    def denominators():
        for one in fetches[2:]:
            one.wait()
        occ_count = eocc_ref.shape[0]
        levels = jnp.broadcast_to(eocc_ref[...].reshape(1, occ_count), (pairs, occ_count)).T
        spots = lax.broadcasted_iota(jnp.int32, levels.shape, 0)
        energy = [jnp.sum(jnp.where(spots == occ_ref[i : i + 1, :], levels, 0.0), axis=0, keepdims=True) for i in (0, 1)]
        pair[core] = jnp.broadcast_to(energy[0] + energy[1], (pairs, pairs)).T
        pair_copy.start()
        virtual = evir_ref[...].reshape(1, evir_ref.shape[0])
        spots = lax.broadcasted_iota(jnp.int32, virtual.shape, 1)
        count = half // virtual.shape[1]
        lead = off_ref[0] + (2 * z + core) * count
        vir[...] = jnp.concatenate(
            [jnp.sum(jnp.where(spots == lead + a, virtual, 0.0), axis=1, keepdims=True) + virtual for a in range(count)],
            axis=1,
        )

    def split_amps():
        share.wait_recv()
        pair_copy.wait_recv()
        for a in range(DEPTH):
            ahead = (a - z + DEPTH) % DEPTH
            amps[a] = slabs[jnp.where(ahead <= REACH * down_blocks(z), zero + ahead, ahead - 1)]
        for i, c in enumerate((core, 1 - core)):
            full = amps[:, c].reshape(pairs, amps.shape[3])
            high = full.astype(jnp.bfloat16)
            both[i * pairs : (i + 1) * pairs, :] = high
            both[(2 + i) * pairs : (3 + i) * pairs, :] = (full - high.astype(jnp.float32)).astype(jnp.bfloat16)

    def compute(k):
        cols = pl.ds(begins[k], PARTS[k])
        block = jnp.concatenate(
            [rows[p, turn(i - x), turn(j - y), :, :, cols].reshape(-1, PARTS[k]) for p in panels for i in range(SIDE) for j in range(SIDE)],
            axis=0,
        )
        high = block.astype(jnp.bfloat16)
        low = (block - high.astype(jnp.float32)).astype(jnp.bfloat16)
        head = jnp.dot(both[...], high, preferred_element_type=jnp.float32)
        tail = jnp.dot(both[: 2 * pairs, :], low, preferred_element_type=jnp.float32)
        ladder = head[: 2 * pairs] + (head[2 * pairs :] + tail)
        stage[:, cols] = ladder[pairs:] / (pair[1 - core][:, 0:1] - vir[:, cols])
        result(k).start()
        spot = pl.ds(pl.multiple_of(mine + begins[k], 128), PARTS[k])
        out_ref[:, spot] = ladder[:pairs] / (pair[core][:, 0:1] - vir[:, cols])

    def send_others(k):
        for p in panels:
            for step in (1, -1):
                others(k, p, step).start()

    def send_line_onward(k):
        if k == 1:
            for p in panels:
                own_arrived(1, p, 1, core)
        for p in panels:
            others_arrived(k, p, core)
            line_onward(k, p).start()

    def finish(k):
        if k == 1:
            for p in panels:
                own_arrived(1, p, 1, 1 - core)
        for p in panels:
            others_arrived(k, p, 1 - core)
            line_onward(k, p).wait_recv()
        compute(k)

    halves.start()
    for axis in (0, 1):
        for step in (1, -1):
            for cc in (0, 1):
                own_direct(axis, step, cc).start()
    fetches[1].wait()
    width = amp_ref.shape[2]
    for p in panels:
        slabs[zero, core, :, p * width : (p + 1) * width] = amp_ref[:, p, :]
    own_slab.start()
    fetches[0].wait()
    halves.wait_recv()
    for p in panels:
        for step in (1, -1):
            own(1, p, 0, step).start()
    for axis in (0, 1):
        own_direct_arrived(axis, core)
    for p in panels:
        onward(0, p).start()
    for p in panels:
        for step in (1, -1):
            own(1, p, 1, step).start()

    def line_point(point):
        for s in range(LAST + 1):
            if POINTS[s] == point:
                line_step(s)

    line_point(0)
    denominators()
    for axis in (0, 1):
        own_direct_arrived(axis, 1 - core)
    for p in panels:
        onward(0, p).wait_recv()
    send_others(0)
    for p in panels:
        own_arrived(1, p, 0, core)
        onward(1, p).start()
    line_point(1)
    send_line_onward(0)
    for p in panels:
        own_arrived(1, p, 0, 1 - core)
        onward(1, p).wait_recv()
    send_others(1)
    line_point(2)
    count = len(PARTS)
    finished = 0
    send_others(2)
    for k in range(1, count):
        send_line_onward(k)
        if k + 2 < count:
            send_others(k + 2)
        line_point(k + 2)
        if k + 2 == POINTS[LAST]:
            split_amps()
        if k + 2 >= POINTS[LAST]:
            while finished <= k - 2:
                finish(finished)
                finished += 1
    while finished < count:
        finish(finished)
        finished += 1

    for block in (rows.at[:, :, 0:3], rows.at[0, 0:3, 0:2]):
        remote(block, block, send.at[0], side.at[0], sibling).wait_send()
    for one in (halves, own_slab, pair_copy, share):
        one.wait_send()
    for d in range(1, REACH + 1):
        pl.when(jnp.logical_or(sends_slab(d), seam_to(d)))(slab_copy(d).wait_send)
    for s in range(1, LAST):
        pl.when(sends_block(s))(block_copy(s).wait_send)
    all_results = remote(stage, out_ref.at[:, pl.ds(mine, half)], send.at[5], side.at[4], sibling)
    all_results.wait_send()
    all_results.wait_recv()


def store_kernel(src_ref, dst_ref, sems):
    count = sems.shape[0]
    height = src_ref.shape[0] // count
    copies = [
        pltpu.make_async_copy(src_ref.at[pl.ds(i * height, height)], dst_ref.at[pl.ds(i * height, height)], sems.at[i])
        for i in range(count)
    ]
    for one in copies:
        one.start()
    for one in copies:
        one.wait()


def gather_and_contract(amplitudes, integrals, occ_pairs, eps_occ, eps_vir, vir_offset, cid=0, name="gather_and_contract"):
    panels, depth, ab = integrals.shape
    mine, _, panel = amplitudes.shape
    pairs = occ_pairs.shape[0]
    cd = panels * panel
    half = ab // 2
    hbm = pl.BlockSpec(memory_space=pltpu.HBM)
    arrays = (amplitudes, integrals, occ_pairs.T, eps_occ, eps_vir)
    return pl.pallas_call(
        gather_kernel,
        out_shape=pltpu.VMEM((pairs, ab), jnp.float32),
        in_specs=[hbm] * 5 + [pl.BlockSpec(memory_space=pltpu.SMEM)],
        out_specs=pl.BlockSpec(memory_space=pltpu.VMEM),
        scratch_shapes=[
            pltpu.VMEM((panels, SIDE, SIDE, 2, depth, half), jnp.float32),
            pltpu.VMEM((2 * DEPTH - 1, 2, mine, cd), jnp.float32),
            pltpu.VMEM((DEPTH, 2, mine, cd), jnp.float32),
            pltpu.VMEM((4 * pairs, cd), jnp.bfloat16),
            pltpu.VMEM((2, pairs, pairs), jnp.float32),
            pltpu.VMEM((1, half), jnp.float32),
            pltpu.VMEM((pairs, half), jnp.float32),
            pltpu.VMEM(amplitudes.shape, jnp.float32),
            pltpu.VMEM((2, pairs), jnp.int32),
            pltpu.VMEM(eps_occ.shape, jnp.float32),
            pltpu.VMEM(eps_vir.shape, jnp.float32),
            pltpu.SemaphoreType.DMA((5,)),
            pltpu.SemaphoreType.DMA((6,)),
            pltpu.SemaphoreType.DMA((len(PIECES), 2, 2, 2)),
            pltpu.SemaphoreType.DMA((len(PIECES), 2)),
            pltpu.SemaphoreType.DMA((len(PARTS), 2, 2)),
            pltpu.SemaphoreType.DMA((len(PARTS), 2)),
            pltpu.SemaphoreType.DMA((REACH + LAST - 1,)),
            pltpu.SemaphoreType.DMA((REACH + LAST - 1,)),
            pltpu.SemaphoreType.DMA((5,)),
            pltpu.SemaphoreType.REGULAR,
        ],
        compiler_params=pltpu.CompilerParams(
            collective_id=cid, has_side_effects=True, vmem_limit_bytes=40 * 1024 * 1024
        ),
        cost_estimate=pl.CostEstimate(
            flops=2 * pairs * cd * ab * 3, bytes_accessed=4 * (pairs * ab + panels * depth * ab), transcendentals=0
        ),
        name=name,
    )(*(pltpu.with_memory_space_constraint(a, pltpu.HBM) for a in arrays), vir_offset)


def shards(amplitudes, integrals, occ_pairs, eps_occ, eps_vir, vir_offset):
    update = gather_and_contract(amplitudes, integrals, occ_pairs, eps_occ, eps_vir, vir_offset)
    return pl.pallas_call(
        store_kernel,
        out_shape=jax.ShapeDtypeStruct(update.shape, jnp.float32),
        in_specs=[pl.BlockSpec(memory_space=pltpu.VMEM)],
        out_specs=pl.BlockSpec(memory_space=pl.ANY),
        scratch_shapes=[pltpu.SemaphoreType.DMA((8,))],
        cost_estimate=pl.CostEstimate(flops=0, bytes_accessed=4 * update.size, transcendentals=0),
        name="store",
    )(pltpu.with_memory_space_constraint(update, pltpu.VMEM))


def solution(mesh):
    return jax.shard_map(
        shards,
        mesh=mesh,
        in_specs=(
            P(("row", "col"), None, None),
            P(None, "row", "col"),
            P("row", None),
            P(),
            P(),
            P(),
        ),
        out_specs=P("row", "col"),
        check_vma=False,
    )
```

```python
import functools

import jax
import jax.numpy as jnp
from jax import lax
from jax.experimental import pallas as pl
from jax.experimental.pallas import tpu as pltpu
from jax.sharding import PartitionSpec as P

MESH = pl.DeviceIdType.MESH
SIDE = 4
DEPTH = 16
REACH = 3
LAST = 4
PIECES = (640, 2560)
PARTS = (640, 1024, 1024, 512)
POINTS = (0, 1, 2, 3, 4)


def gather_kernel(
    amp_hbm, int_hbm, occ_hbm, eocc_hbm, evir_hbm, off_ref, out_ref,
    shard, rows, slabs, amps, both, pair, vir, stage,
    amp_ref, occ_ref, eocc_ref, evir_ref,
    local, send, near, onto, far, over, line_send, line_got, side, ready,
):
    row, z = lax.axis_index("row"), lax.axis_index("col")
    x, y, core = row // 8, (row // 2) % SIDE, row % 2
    way = 1 - 2 * core
    half = int_hbm.shape[2] // 2
    mine = pl.multiple_of(core * half, 128)
    pairs = out_ref.shape[0]
    panels = (0, 1)

    def turn(v):
        return (v + SIDE) % SIDE

    def beside(axis, step, cc):
        if axis == 0:
            return {"row": (turn(x + step) * SIDE + y) * 2 + cc, "col": z}
        return {"row": (x * SIDE + turn(y + step)) * 2 + cc, "col": z}

    sibling = {"row": row + way, "col": z}

    zero = DEPTH - 1
    blocks = zero // REACH

    def down_blocks(v):
        return jnp.where(v + 2 * REACH <= zero, 2, 1)

    def blocks_at(v):
        return jnp.where(core == 0, blocks - down_blocks(v), down_blocks(v))

    def on_line(d):
        return {"row": row, "col": (z + d + DEPTH) % DEPTH}

    def target(d):
        return z + way * d

    def sends(d, count):
        inside = jnp.logical_or(core == 0, target(d) >= 0)
        return jnp.logical_and(inside, blocks_at((target(d) + DEPTH) % DEPTH) >= count)

    def sends_slab(d):
        return sends(d, 1)

    def gets_slab(d):
        return jnp.logical_or(core == 0, z + d <= zero)

    def seam_to(d):
        return jnp.logical_and(core == 1, z < d)

    def seam_from(d):
        return jnp.logical_and(core == 1, z + d > zero)

    def sends_block(s):
        return sends(REACH, s + 1)

    def gets_block(s):
        return blocks_at(z) >= s + 1

    def fetch(i, src, dst):
        return pltpu.make_async_copy(src, dst, local.at[i])

    fetches = [
        fetch(0, int_hbm, shard),
        fetch(1, amp_hbm, amp_ref),
        fetch(2, occ_hbm, occ_ref),
        fetch(3, eocc_hbm, eocc_ref),
        fetch(4, evir_hbm, evir_ref),
    ]
    for one in fetches:
        one.start()

    barrier = pltpu.get_barrier_semaphore()

    def greet(to):
        pl.semaphore_signal(barrier, inc=1, device_id=to, device_id_type=MESH)

    greeted = 9
    greet(sibling)
    for axis in (0, 1):
        for step in (1, -1):
            for cc in (0, 1):
                greet(beside(axis, step, cc))
    for d in range(1, REACH + 1):
        pl.when(gets_slab(d))(functools.partial(greet, on_line(-way * d)))
        pl.when(seam_to(d))(functools.partial(greet, on_line(way * d)))
        greeted = greeted + sends_slab(d).astype(jnp.int32) + seam_from(d).astype(jnp.int32)
    pl.semaphore_wait(barrier, greeted)

    def tell(to):
        pl.semaphore_signal(ready, inc=1, device_id=to, device_id_type=MESH)

    for d in range(1, REACH + 1):
        pl.when(seam_from(d))(functools.partial(tell, on_line(-way * d)))

    def remote(src, dst, sent, got, to):
        return pltpu.make_async_remote_copy(
            src_ref=src, dst_ref=dst, send_sem=sent, recv_sem=got, device_id=to, device_id_type=MESH
        )

    starts = [sum(PIECES[:a]) for a in range(len(PIECES))]
    begins = [sum(PARTS[:k]) for k in range(len(PARTS))]

    def place(p, along_first, along_second, cols):
        if p == 0:
            return rows.at[0, along_first, along_second, :, :, cols]
        return rows.at[1, along_second, along_first, :, :, cols]

    def own_direct(axis, step, cc):
        src = shard.at[:, :, pl.ds(pl.multiple_of(cc * half, 128), PIECES[0])]
        back = (-step) % SIDE
        spot = (slice(None), back, 0) if axis == 0 else (slice(None), 0, back)
        dst = rows.at[(*spot, core, slice(None), pl.ds(0, PIECES[0]))]
        return remote(src, dst, send.at[0], near.at[0, axis, 0, (1 - step) // 2], beside(axis, step, cc))

    def own_direct_arrived(axis, index):
        block = rows.at[:, 0, 0, :, :, pl.ds(0, PIECES[0])]
        remote(block, block, send.at[0], near.at[0, axis, 0, index], sibling).wait_recv()

    def own(a, p, phase, step):
        cols = pl.ds(starts[a], PIECES[a])
        back = (-step) % SIDE
        dst = place(p, back, 0, cols) if phase == 0 else place(p, 0, back, cols)
        axis = phase if p == 0 else 1 - phase
        return remote(place(p, 0, 0, cols), dst, send.at[0], near.at[a, p, phase, (1 - step) // 2], beside(axis, step, core))

    def own_arrived(a, p, phase, index):
        block = place(p, 0, 0, pl.ds(starts[a], PIECES[a]))
        remote(block, block, send.at[0], near.at[a, p, phase, index], sibling).wait_recv()

    def onward(a, p):
        cols = pl.ds(starts[a], PIECES[a])
        return remote(place(p, turn(-way), 0, cols), place(p, 2, 0, cols), send.at[0], onto.at[a, p], beside(p, way, core))

    def others(k, p, step):
        cols = pl.ds(begins[k], PARTS[k])
        three = pl.ds(1, SIDE - 1)
        return remote(
            place(p, three, 0, cols), place(p, three, (-step) % SIDE, cols),
            send.at[0], far.at[k, p, (1 - step) // 2], beside(1 - p, step, core),
        )

    def others_arrived(k, p, index):
        block = place(p, pl.ds(1, SIDE - 1), 0, pl.ds(begins[k], PARTS[k]))
        remote(block, block, send.at[0], far.at[k, p, index], sibling).wait_recv()

    def line_onward(k, p):
        cols = pl.ds(begins[k], PARTS[k])
        whole = pl.ds(0, SIDE)
        return remote(place(p, whole, turn(-way), cols), place(p, whole, 2, cols), send.at[0], over.at[k, p], beside(1 - p, way, core))

    def slab_block(s):
        low = zero - REACH * s if s > 0 else zero
        return slabs.at[pl.ds(low + core * (2 * (zero - low) - REACH + 1), REACH)]

    def slab_copy(d):
        return remote(slabs.at[zero], slabs.at[zero - way * d], line_send.at[d - 1], line_got.at[d - 1], on_line(way * d))

    def block_copy(s):
        i = REACH + s - 1
        return remote(slab_block(s), slab_block(s + 1), line_send.at[i], line_got.at[i], on_line(way * REACH))

    def line_step(s):
        if s == 0:
            own_slab.wait_recv()
            for d in range(1, REACH + 1):
                pl.when(sends_slab(d))(slab_copy(d).start)
            return
        if s == 1:
            for d in range(1, REACH + 1):
                pl.when(gets_slab(d))(slab_copy(d).wait_recv)
        else:
            pl.when(gets_block(s - 1))(block_copy(s - 1).wait_recv)
        if s == 2:
            late = sum(seam_to(d).astype(jnp.int32) for d in range(1, REACH + 1))
            pl.when(late > 0)(functools.partial(pl.semaphore_wait, ready, late))
            for d in range(1, REACH + 1):
                pl.when(seam_to(d))(slab_copy(d).start)
        if s < LAST:
            pl.when(sends_block(s))(block_copy(s).start)
        else:
            for d in range(1, REACH + 1):
                pl.when(seam_from(d))(slab_copy(d).wait_recv)
            share.start()

    halves = remote(
        shard.at[:, :, pl.ds(pl.multiple_of((1 - core) * half, 128), half)],
        rows.at[:, 0, 0, core], send.at[1], side.at[0], sibling,
    )
    own_slab = remote(slabs.at[zero, core], slabs.at[zero, core], send.at[2], side.at[1], sibling)
    pair_copy = remote(pair.at[core], pair.at[core], send.at[3], side.at[2], sibling)
    side_slabs = slabs.at[pl.ds(core * DEPTH, zero)]
    share = remote(side_slabs, side_slabs, send.at[4], side.at[3], sibling)

    def result(k):
        block = out_ref.at[:, pl.ds(pl.multiple_of(mine + begins[k], 128), PARTS[k])]
        return remote(stage.at[:, pl.ds(begins[k], PARTS[k])], block, send.at[5], side.at[4], sibling)

    def denominators():
        for one in fetches[2:]:
            one.wait()
        occ_count = eocc_ref.shape[0]
        levels = jnp.broadcast_to(eocc_ref[...].reshape(1, occ_count), (pairs, occ_count)).T
        spots = lax.broadcasted_iota(jnp.int32, levels.shape, 0)
        energy = [jnp.sum(jnp.where(spots == occ_ref[i : i + 1, :], levels, 0.0), axis=0, keepdims=True) for i in (0, 1)]
        pair[core] = jnp.broadcast_to(energy[0] + energy[1], (pairs, pairs)).T
        pair_copy.start()
        virtual = evir_ref[...].reshape(1, evir_ref.shape[0])
        spots = lax.broadcasted_iota(jnp.int32, virtual.shape, 1)
        count = half // virtual.shape[1]
        lead = off_ref[0] + (2 * z + core) * count
        vir[...] = jnp.concatenate(
            [jnp.sum(jnp.where(spots == lead + a, virtual, 0.0), axis=1, keepdims=True) + virtual for a in range(count)],
            axis=1,
        )

    def split_amps():
        share.wait_recv()
        pair_copy.wait_recv()
        for a in range(DEPTH):
            ahead = (a - z + DEPTH) % DEPTH
            amps[a] = slabs[jnp.where(ahead <= REACH * down_blocks(z), zero + ahead, ahead - 1)]
        for i, c in enumerate((core, 1 - core)):
            full = amps[:, c].reshape(pairs, amps.shape[3])
            high = full.astype(jnp.bfloat16)
            both[i * pairs : (i + 1) * pairs, :] = high
            both[(2 + i) * pairs : (3 + i) * pairs, :] = (full - high.astype(jnp.float32)).astype(jnp.bfloat16)

    def compute(k):
        cols = pl.ds(begins[k], PARTS[k])
        block = jnp.concatenate(
            [rows[p, turn(i - x), turn(j - y), :, :, cols].reshape(-1, PARTS[k]) for p in panels for i in range(SIDE) for j in range(SIDE)],
            axis=0,
        )
        high = block.astype(jnp.bfloat16)
        low = (block - high.astype(jnp.float32)).astype(jnp.bfloat16)
        head = jnp.dot(both[...], high, preferred_element_type=jnp.float32)
        tail = jnp.dot(both[: 2 * pairs, :], low, preferred_element_type=jnp.float32)
        ladder = head[: 2 * pairs] + (head[2 * pairs :] + tail)
        stage[:, cols] = ladder[pairs:] / (pair[1 - core][:, 0:1] - vir[:, cols])
        result(k).start()
        spot = pl.ds(pl.multiple_of(mine + begins[k], 128), PARTS[k])
        out_ref[:, spot] = ladder[:pairs] / (pair[core][:, 0:1] - vir[:, cols])

    def send_others(k):
        for p in panels:
            for step in (1, -1):
                others(k, p, step).start()

    def send_line_onward(k):
        if k == 1:
            for p in panels:
                own_arrived(1, p, 1, core)
        for p in panels:
            others_arrived(k, p, core)
            line_onward(k, p).start()

    def finish(k):
        if k == 1:
            for p in panels:
                own_arrived(1, p, 1, 1 - core)
        for p in panels:
            others_arrived(k, p, 1 - core)
            line_onward(k, p).wait_recv()
        compute(k)

    fetches[0].wait()
    for axis in (0, 1):
        for step in (1, -1):
            for cc in (0, 1):
                own_direct(axis, step, cc).start()
        if axis == 0:
            halves.start()
    keep = pltpu.make_async_copy(shard.at[:, :, pl.ds(mine, half)], rows.at[:, 0, 0, core], local.at[0])
    keep.start()
    fetches[1].wait()
    width = amp_ref.shape[2]
    for p in panels:
        slabs[zero, core, :, p * width : (p + 1) * width] = amp_ref[:, p, :]
    own_slab.start()
    keep.wait()
    halves.wait_recv()
    for p in panels:
        for step in (1, -1):
            own(1, p, 0, step).start()
    for axis in (0, 1):
        own_direct_arrived(axis, core)
    for p in panels:
        onward(0, p).start()
    for p in panels:
        for step in (1, -1):
            own(1, p, 1, step).start()

    def line_point(point):
        for s in range(LAST + 1):
            if POINTS[s] == point:
                line_step(s)

    line_point(0)
    denominators()
    for axis in (0, 1):
        own_direct_arrived(axis, 1 - core)
    for p in panels:
        onward(0, p).wait_recv()
    send_others(0)
    for p in panels:
        own_arrived(1, p, 0, core)
        onward(1, p).start()
    line_point(1)
    send_line_onward(0)
    for p in panels:
        own_arrived(1, p, 0, 1 - core)
        onward(1, p).wait_recv()
    send_others(1)
    line_point(2)
    count = len(PARTS)
    finished = 0
    send_others(2)
    for k in range(1, count):
        send_line_onward(k)
        if k + 2 < count:
            send_others(k + 2)
        line_point(k + 2)
        if k + 2 == POINTS[LAST]:
            split_amps()
        if k + 2 >= POINTS[LAST]:
            while finished <= k - 2:
                finish(finished)
                finished += 1
    while finished < count:
        finish(finished)
        finished += 1

    for block in (rows.at[:, :, 0:3], rows.at[0, 0:3, 0:2]):
        remote(block, block, send.at[0], side.at[0], sibling).wait_send()
    for one in (halves, own_slab, pair_copy, share):
        one.wait_send()
    for d in range(1, REACH + 1):
        pl.when(jnp.logical_or(sends_slab(d), seam_to(d)))(slab_copy(d).wait_send)
    for s in range(1, LAST):
        pl.when(sends_block(s))(block_copy(s).wait_send)
    all_results = remote(stage, out_ref.at[:, pl.ds(mine, half)], send.at[5], side.at[4], sibling)
    all_results.wait_send()
    all_results.wait_recv()


def store_kernel(src_ref, dst_ref, sems):
    count = sems.shape[0]
    height = src_ref.shape[0] // count
    copies = [
        pltpu.make_async_copy(src_ref.at[pl.ds(i * height, height)], dst_ref.at[pl.ds(i * height, height)], sems.at[i])
        for i in range(count)
    ]
    for one in copies:
        one.start()
    for one in copies:
        one.wait()


def gather_and_contract(amplitudes, integrals, occ_pairs, eps_occ, eps_vir, vir_offset, cid=0, name="gather_and_contract"):
    panels, depth, ab = integrals.shape
    mine, _, panel = amplitudes.shape
    pairs = occ_pairs.shape[0]
    cd = panels * panel
    half = ab // 2
    hbm = pl.BlockSpec(memory_space=pltpu.HBM)
    arrays = (amplitudes, integrals, occ_pairs.T, eps_occ, eps_vir)
    return pl.pallas_call(
        gather_kernel,
        out_shape=pltpu.VMEM((pairs, ab), jnp.float32),
        in_specs=[hbm] * 5 + [pl.BlockSpec(memory_space=pltpu.SMEM)],
        out_specs=pl.BlockSpec(memory_space=pltpu.VMEM),
        scratch_shapes=[
            pltpu.VMEM(integrals.shape, jnp.float32),
            pltpu.VMEM((panels, SIDE, SIDE, 2, depth, half), jnp.float32),
            pltpu.VMEM((2 * DEPTH - 1, 2, mine, cd), jnp.float32),
            pltpu.VMEM((DEPTH, 2, mine, cd), jnp.float32),
            pltpu.VMEM((4 * pairs, cd), jnp.bfloat16),
            pltpu.VMEM((2, pairs, pairs), jnp.float32),
            pltpu.VMEM((1, half), jnp.float32),
            pltpu.VMEM((pairs, half), jnp.float32),
            pltpu.VMEM(amplitudes.shape, jnp.float32),
            pltpu.VMEM((2, pairs), jnp.int32),
            pltpu.VMEM(eps_occ.shape, jnp.float32),
            pltpu.VMEM(eps_vir.shape, jnp.float32),
            pltpu.SemaphoreType.DMA((5,)),
            pltpu.SemaphoreType.DMA((6,)),
            pltpu.SemaphoreType.DMA((len(PIECES), 2, 2, 2)),
            pltpu.SemaphoreType.DMA((len(PIECES), 2)),
            pltpu.SemaphoreType.DMA((len(PARTS), 2, 2)),
            pltpu.SemaphoreType.DMA((len(PARTS), 2)),
            pltpu.SemaphoreType.DMA((REACH + LAST - 1,)),
            pltpu.SemaphoreType.DMA((REACH + LAST - 1,)),
            pltpu.SemaphoreType.DMA((5,)),
            pltpu.SemaphoreType.REGULAR,
        ],
        compiler_params=pltpu.CompilerParams(
            collective_id=cid, has_side_effects=True, vmem_limit_bytes=40 * 1024 * 1024
        ),
        cost_estimate=pl.CostEstimate(
            flops=2 * pairs * cd * ab * 3, bytes_accessed=4 * (pairs * ab + panels * depth * ab), transcendentals=0
        ),
        name=name,
    )(*(pltpu.with_memory_space_constraint(a, pltpu.HBM) for a in arrays), vir_offset)


def shards(amplitudes, integrals, occ_pairs, eps_occ, eps_vir, vir_offset):
    update = gather_and_contract(amplitudes, integrals, occ_pairs, eps_occ, eps_vir, vir_offset)
    return pl.pallas_call(
        store_kernel,
        out_shape=jax.ShapeDtypeStruct(update.shape, jnp.float32),
        in_specs=[pl.BlockSpec(memory_space=pltpu.VMEM)],
        out_specs=pl.BlockSpec(memory_space=pl.ANY),
        scratch_shapes=[pltpu.SemaphoreType.DMA((8,))],
        cost_estimate=pl.CostEstimate(flops=0, bytes_accessed=4 * update.size, transcendentals=0),
        name="store",
    )(pltpu.with_memory_space_constraint(update, pltpu.VMEM))


def solution(mesh):
    return jax.shard_map(
        shards,
        mesh=mesh,
        in_specs=(
            P(("row", "col"), None, None),
            P(None, "row", "col"),
            P("row", None),
            P(),
            P(),
            P(),
        ),
        out_specs=P("row", "col"),
        check_vma=False,
    )
```

```python
import functools

import jax
import jax.numpy as jnp
from jax import lax
from jax.experimental import pallas as pl
from jax.experimental.pallas import tpu as pltpu
from jax.sharding import PartitionSpec as P

MESH = pl.DeviceIdType.MESH
SIDE = 4
DEPTH = 16
REACH = 4
LAST = 3
GATE = 8
PIECES = (640, 2560)
PARTS = (640, 1024, 1024, 512)
POINTS = (0, 1, 2, 4)


def gather_kernel(
    amp_hbm, int_hbm, occ_hbm, eocc_hbm, evir_hbm, off_ref, out_ref,
    shard, rows, slabs, amps, both, pair, vir, stage,
    amp_ref, occ_ref, eocc_ref, evir_ref,
    local, send, near, onto, far, over, line_send, line_got, side, ready,
):
    row, z = lax.axis_index("row"), lax.axis_index("col")
    x, y, core = row // 8, (row // 2) % SIDE, row % 2
    way = 1 - 2 * core
    half = int_hbm.shape[2] // 2
    mine = pl.multiple_of(core * half, 128)
    pairs = out_ref.shape[0]
    panels = (0, 1)

    def turn(v):
        return (v + SIDE) % SIDE

    def beside(axis, step, cc):
        if axis == 0:
            return {"row": (turn(x + step) * SIDE + y) * 2 + cc, "col": z}
        return {"row": (x * SIDE + turn(y + step)) * 2 + cc, "col": z}

    sibling = {"row": row + way, "col": z}

    zero = DEPTH - 1
    blocks = -(-zero // REACH)

    def down_blocks(v):
        return jnp.where(v + 2 * REACH <= zero, 2, 1)

    def blocks_at(v):
        return jnp.where(core == 0, blocks - down_blocks(v), down_blocks(v))

    def on_line(d):
        return {"row": row, "col": (z + d + DEPTH) % DEPTH}

    def gated(v, d):
        first = jnp.logical_and(v == 0, row == 0)
        up = jnp.logical_and(jnp.logical_and(v >= 0, v < GATE), jnp.logical_and(v + d <= zero, jnp.logical_not(first)))
        return jnp.where(core == 0, up, jnp.logical_and(v < d, v >= 0))

    def gated_to(d):
        return gated(z, d)

    def gated_from(d):
        return gated(jnp.where(core == 0, z - d, (z + d) % DEPTH), d)

    def sends_block(s):
        inside = jnp.logical_or(core == 0, z >= REACH)
        return jnp.logical_and(inside, blocks_at((z + way * REACH + DEPTH) % DEPTH) > s)

    def gets_block(s):
        return blocks_at(z) > s

    relays = jnp.logical_and(core == 0, sends_block(2))

    def fetch(i, src, dst):
        return pltpu.make_async_copy(src, dst, local.at[i])

    fetches = [
        fetch(0, int_hbm, shard),
        fetch(1, amp_hbm, amp_ref),
        fetch(2, occ_hbm, occ_ref),
        fetch(3, eocc_hbm, eocc_ref),
        fetch(4, evir_hbm, evir_ref),
    ]
    for one in fetches:
        one.start()

    barrier = pltpu.get_barrier_semaphore()

    def greet(to):
        pl.semaphore_signal(barrier, inc=1, device_id=to, device_id_type=MESH)

    greeted = 9
    greet(sibling)
    for axis in (0, 1):
        for step in (1, -1):
            for cc in (0, 1):
                greet(beside(axis, step, cc))
    for d in range(1, REACH + 1):
        pl.when(gated_to(d))(functools.partial(greet, on_line(way * d)))
        pl.when(jnp.logical_not(gated_from(d)))(functools.partial(greet, on_line(-way * d)))
        greeted = greeted + gated_from(d).astype(jnp.int32) + 1 - gated_to(d).astype(jnp.int32)
    pl.semaphore_wait(barrier, greeted)

    def tell(to):
        pl.semaphore_signal(ready, inc=1, device_id=to, device_id_type=MESH)

    for d in range(1, REACH + 1):
        pl.when(gated_from(d))(functools.partial(tell, on_line(-way * d)))

    def remote(src, dst, sent, got, to):
        return pltpu.make_async_remote_copy(
            src_ref=src, dst_ref=dst, send_sem=sent, recv_sem=got, device_id=to, device_id_type=MESH
        )

    starts = [sum(PIECES[:a]) for a in range(len(PIECES))]
    begins = [sum(PARTS[:k]) for k in range(len(PARTS))]

    def place(p, along_first, along_second, cols):
        if p == 0:
            return rows.at[0, along_first, along_second, :, :, cols]
        return rows.at[1, along_second, along_first, :, :, cols]

    def own_direct(axis, step, cc):
        src = shard.at[:, :, pl.ds(pl.multiple_of(cc * half, 128), PIECES[0])]
        back = (-step) % SIDE
        spot = (slice(None), back, 0) if axis == 0 else (slice(None), 0, back)
        dst = rows.at[(*spot, core, slice(None), pl.ds(0, PIECES[0]))]
        return remote(src, dst, send.at[0], near.at[0, axis, 0, (1 - step) // 2], beside(axis, step, cc))

    def own_direct_arrived(axis, index):
        block = rows.at[:, 0, 0, :, :, pl.ds(0, PIECES[0])]
        remote(block, block, send.at[0], near.at[0, axis, 0, index], sibling).wait_recv()

    def own(a, p, phase, step):
        cols = pl.ds(starts[a], PIECES[a])
        back = (-step) % SIDE
        dst = place(p, back, 0, cols) if phase == 0 else place(p, 0, back, cols)
        axis = phase if p == 0 else 1 - phase
        return remote(place(p, 0, 0, cols), dst, send.at[0], near.at[a, p, phase, (1 - step) // 2], beside(axis, step, core))

    def own_arrived(a, p, phase, index):
        block = place(p, 0, 0, pl.ds(starts[a], PIECES[a]))
        remote(block, block, send.at[0], near.at[a, p, phase, index], sibling).wait_recv()

    def onward(a, p):
        cols = pl.ds(starts[a], PIECES[a])
        return remote(place(p, turn(-way), 0, cols), place(p, 2, 0, cols), send.at[0], onto.at[a, p], beside(p, way, core))

    def others(k, p, step):
        cols = pl.ds(begins[k], PARTS[k])
        three = pl.ds(1, SIDE - 1)
        return remote(
            place(p, three, 0, cols), place(p, three, (-step) % SIDE, cols),
            send.at[0], far.at[k, p, (1 - step) // 2], beside(1 - p, step, core),
        )

    def others_arrived(k, p, index):
        block = place(p, pl.ds(1, SIDE - 1), 0, pl.ds(begins[k], PARTS[k]))
        remote(block, block, send.at[0], far.at[k, p, index], sibling).wait_recv()

    def line_onward(k, p):
        cols = pl.ds(begins[k], PARTS[k])
        whole = pl.ds(0, SIDE)
        return remote(place(p, whole, turn(-way), cols), place(p, whole, 2, cols), send.at[0], over.at[k, p], beside(1 - p, way, core))

    def slab_block(s):
        low = zero - REACH * s if s > 0 else zero
        return slabs.at[pl.ds(low + core * (2 * (zero - low) - REACH + 1), REACH)]

    def slab_copy(d):
        return remote(slabs.at[zero], slabs.at[zero - way * d], line_send.at[d - 1], line_got.at[d - 1], on_line(way * d))

    def block_copy(s):
        i = REACH + s - 1
        return remote(slab_block(s), slab_block(s + 1), line_send.at[i], line_got.at[i], on_line(way * REACH))

    def send_gated():
        late = sum(gated_to(d).astype(jnp.int32) for d in range(1, REACH + 1))
        pl.when(late > 0)(functools.partial(pl.semaphore_wait, ready, late))
        for d in range(1, REACH + 1):
            pl.when(gated_to(d))(slab_copy(d).start)

    def line_step(s):
        if s == 0:
            own_slab.wait_recv()
            for d in range(1, REACH + 1):
                pl.when(jnp.logical_not(gated_to(d)))(slab_copy(d).start)
            pl.when(core == 0)(send_gated)
        if s == 1:
            for d in range(1, REACH + 1):
                pl.when(jnp.logical_or(core == 0, z + d <= zero))(slab_copy(d).wait_recv)
            pl.when(sends_block(1))(block_copy(1).start)
        if s == 2:
            pl.when(core == 1)(send_gated)
            pl.when(relays)(block_copy(1).wait_recv)
            pl.when(sends_block(2))(block_copy(2).start)
        if s == LAST:
            pl.when(jnp.logical_and(gets_block(1), jnp.logical_not(relays)))(block_copy(1).wait_recv)
            pl.when(gets_block(2))(block_copy(2).wait_recv)
            for d in range(1, REACH + 1):
                pl.when(jnp.logical_and(core == 1, z + d > zero))(slab_copy(d).wait_recv)
            share.start()

    halves = remote(
        shard.at[:, :, pl.ds(pl.multiple_of((1 - core) * half, 128), half)],
        rows.at[:, 0, 0, core], send.at[1], side.at[0], sibling,
    )
    own_slab = remote(slabs.at[zero, core], slabs.at[zero, core], send.at[2], side.at[1], sibling)
    pair_copy = remote(pair.at[core], pair.at[core], send.at[3], side.at[2], sibling)
    reach = REACH * LAST
    side_slabs = slabs.at[pl.ds(zero - reach + core * (reach + 1), reach)]
    share = remote(side_slabs, side_slabs, send.at[4], side.at[3], sibling)

    def result(k):
        block = out_ref.at[:, pl.ds(pl.multiple_of(mine + begins[k], 128), PARTS[k])]
        return remote(stage.at[:, pl.ds(begins[k], PARTS[k])], block, send.at[5], side.at[4], sibling)

    def denominators():
        for one in fetches[2:]:
            one.wait()
        occ_count = eocc_ref.shape[0]
        levels = jnp.broadcast_to(eocc_ref[...].reshape(1, occ_count), (pairs, occ_count)).T
        spots = lax.broadcasted_iota(jnp.int32, levels.shape, 0)
        energy = [jnp.sum(jnp.where(spots == occ_ref[i : i + 1, :], levels, 0.0), axis=0, keepdims=True) for i in (0, 1)]
        pair[core] = jnp.broadcast_to(energy[0] + energy[1], (pairs, pairs)).T
        pair_copy.start()
        virtual = evir_ref[...].reshape(1, evir_ref.shape[0])
        spots = lax.broadcasted_iota(jnp.int32, virtual.shape, 1)
        count = half // virtual.shape[1]
        lead = off_ref[0] + (2 * z + core) * count
        vir[...] = jnp.concatenate(
            [jnp.sum(jnp.where(spots == lead + a, virtual, 0.0), axis=1, keepdims=True) + virtual for a in range(count)],
            axis=1,
        )

    def split_amps():
        share.wait_recv()
        pair_copy.wait_recv()
        for a in range(DEPTH):
            ahead = (a - z + DEPTH) % DEPTH
            amps[a] = slabs[jnp.where(ahead <= REACH * down_blocks(z), zero + ahead, ahead - 1)]
        for i, c in enumerate((core, 1 - core)):
            full = amps[:, c].reshape(pairs, amps.shape[3])
            high = full.astype(jnp.bfloat16)
            both[i * pairs : (i + 1) * pairs, :] = high
            both[(2 + i) * pairs : (3 + i) * pairs, :] = (full - high.astype(jnp.float32)).astype(jnp.bfloat16)

    def compute(k):
        cols = pl.ds(begins[k], PARTS[k])
        block = jnp.concatenate(
            [rows[p, turn(i - x), turn(j - y), :, :, cols].reshape(-1, PARTS[k]) for p in panels for i in range(SIDE) for j in range(SIDE)],
            axis=0,
        )
        high = block.astype(jnp.bfloat16)
        low = (block - high.astype(jnp.float32)).astype(jnp.bfloat16)
        head = jnp.dot(both[...], high, preferred_element_type=jnp.float32)
        tail = jnp.dot(both[: 2 * pairs, :], low, preferred_element_type=jnp.float32)
        ladder = head[: 2 * pairs] + (head[2 * pairs :] + tail)
        stage[:, cols] = ladder[pairs:] / (pair[1 - core][:, 0:1] - vir[:, cols])
        result(k).start()
        spot = pl.ds(pl.multiple_of(mine + begins[k], 128), PARTS[k])
        out_ref[:, spot] = ladder[:pairs] / (pair[core][:, 0:1] - vir[:, cols])

    def send_others(k):
        for p in panels:
            for step in (1, -1):
                others(k, p, step).start()

    def send_line_onward(k):
        if k == 1:
            for p in panels:
                own_arrived(1, p, 1, core)
        for p in panels:
            others_arrived(k, p, core)
            line_onward(k, p).start()

    def finish(k):
        if k == 1:
            for p in panels:
                own_arrived(1, p, 1, 1 - core)
        for p in panels:
            others_arrived(k, p, 1 - core)
            line_onward(k, p).wait_recv()
        compute(k)

    fetches[0].wait()
    for axis in (0, 1):
        for step in (1, -1):
            for cc in (0, 1):
                own_direct(axis, step, cc).start()
        if axis == 0:
            halves.start()
    keep = pltpu.make_async_copy(shard.at[:, :, pl.ds(mine, half)], rows.at[:, 0, 0, core], local.at[0])
    keep.start()
    fetches[1].wait()
    width = amp_ref.shape[2]
    for p in panels:
        slabs[zero, core, :, p * width : (p + 1) * width] = amp_ref[:, p, :]
    own_slab.start()
    keep.wait()
    halves.wait_recv()
    for p in panels:
        for step in (1, -1):
            own(1, p, 0, step).start()
    for axis in (0, 1):
        own_direct_arrived(axis, core)
    for p in panels:
        onward(0, p).start()
    for p in panels:
        for step in (1, -1):
            own(1, p, 1, step).start()

    def line_point(point):
        for s in range(LAST + 1):
            if POINTS[s] == point:
                line_step(s)

    line_point(0)
    denominators()
    for axis in (0, 1):
        own_direct_arrived(axis, 1 - core)
    for p in panels:
        onward(0, p).wait_recv()
    send_others(0)
    for p in panels:
        own_arrived(1, p, 0, core)
        onward(1, p).start()
    send_line_onward(0)
    line_point(1)
    for p in panels:
        own_arrived(1, p, 0, 1 - core)
        onward(1, p).wait_recv()
    send_others(1)
    line_point(2)
    count = len(PARTS)
    finished = 0
    send_others(2)
    for k in range(1, count):
        send_line_onward(k)
        if k + 2 < count:
            send_others(k + 2)
        line_point(k + 2)
        if k + 2 == POINTS[LAST]:
            split_amps()
        if k + 2 >= POINTS[LAST]:
            while finished <= k - 2:
                finish(finished)
                finished += 1
    while finished < count:
        finish(finished)
        finished += 1

    for block in (rows.at[:, :, 0:3], rows.at[0, 0:3, 0:2]):
        remote(block, block, send.at[0], side.at[0], sibling).wait_send()
    for one in (halves, own_slab, pair_copy, share):
        one.wait_send()
    for d in range(1, REACH + 1):
        slab_copy(d).wait_send()
    for s in range(1, LAST):
        pl.when(sends_block(s))(block_copy(s).wait_send)
    all_results = remote(stage, out_ref.at[:, pl.ds(mine, half)], send.at[5], side.at[4], sibling)
    all_results.wait_send()
    all_results.wait_recv()


def store_kernel(src_ref, dst_ref, sems):
    count = sems.shape[0]
    height = src_ref.shape[0] // count
    copies = [
        pltpu.make_async_copy(src_ref.at[pl.ds(i * height, height)], dst_ref.at[pl.ds(i * height, height)], sems.at[i])
        for i in range(count)
    ]
    for one in copies:
        one.start()
    for one in copies:
        one.wait()


def gather_and_contract(amplitudes, integrals, occ_pairs, eps_occ, eps_vir, vir_offset, cid=0, name="gather_and_contract"):
    panels, depth, ab = integrals.shape
    mine, _, panel = amplitudes.shape
    pairs = occ_pairs.shape[0]
    cd = panels * panel
    half = ab // 2
    hbm = pl.BlockSpec(memory_space=pltpu.HBM)
    arrays = (amplitudes, integrals, occ_pairs.T, eps_occ, eps_vir)
    return pl.pallas_call(
        gather_kernel,
        out_shape=pltpu.VMEM((pairs, ab), jnp.float32),
        in_specs=[hbm] * 5 + [pl.BlockSpec(memory_space=pltpu.SMEM)],
        out_specs=pl.BlockSpec(memory_space=pltpu.VMEM),
        scratch_shapes=[
            pltpu.VMEM(integrals.shape, jnp.float32),
            pltpu.VMEM((panels, SIDE, SIDE, 2, depth, half), jnp.float32),
            pltpu.VMEM((2 * DEPTH - 1, 2, mine, cd), jnp.float32),
            pltpu.VMEM((DEPTH, 2, mine, cd), jnp.float32),
            pltpu.VMEM((4 * pairs, cd), jnp.bfloat16),
            pltpu.VMEM((2, pairs, pairs), jnp.float32),
            pltpu.VMEM((1, half), jnp.float32),
            pltpu.VMEM((pairs, half), jnp.float32),
            pltpu.VMEM(amplitudes.shape, jnp.float32),
            pltpu.VMEM((2, pairs), jnp.int32),
            pltpu.VMEM(eps_occ.shape, jnp.float32),
            pltpu.VMEM(eps_vir.shape, jnp.float32),
            pltpu.SemaphoreType.DMA((5,)),
            pltpu.SemaphoreType.DMA((6,)),
            pltpu.SemaphoreType.DMA((len(PIECES), 2, 2, 2)),
            pltpu.SemaphoreType.DMA((len(PIECES), 2)),
            pltpu.SemaphoreType.DMA((len(PARTS), 2, 2)),
            pltpu.SemaphoreType.DMA((len(PARTS), 2)),
            pltpu.SemaphoreType.DMA((REACH + LAST - 1,)),
            pltpu.SemaphoreType.DMA((REACH + LAST - 1,)),
            pltpu.SemaphoreType.DMA((5,)),
            pltpu.SemaphoreType.REGULAR,
        ],
        compiler_params=pltpu.CompilerParams(
            collective_id=cid, has_side_effects=True, vmem_limit_bytes=40 * 1024 * 1024
        ),
        cost_estimate=pl.CostEstimate(
            flops=2 * pairs * cd * ab * 3, bytes_accessed=4 * (pairs * ab + panels * depth * ab), transcendentals=0
        ),
        name=name,
    )(*(pltpu.with_memory_space_constraint(a, pltpu.HBM) for a in arrays), vir_offset)


def shards(amplitudes, integrals, occ_pairs, eps_occ, eps_vir, vir_offset):
    update = gather_and_contract(amplitudes, integrals, occ_pairs, eps_occ, eps_vir, vir_offset)
    return pl.pallas_call(
        store_kernel,
        out_shape=jax.ShapeDtypeStruct(update.shape, jnp.float32),
        in_specs=[pl.BlockSpec(memory_space=pltpu.VMEM)],
        out_specs=pl.BlockSpec(memory_space=pl.ANY),
        scratch_shapes=[pltpu.SemaphoreType.DMA((8,))],
        cost_estimate=pl.CostEstimate(flops=0, bytes_accessed=4 * update.size, transcendentals=0),
        name="store",
    )(pltpu.with_memory_space_constraint(update, pltpu.VMEM))


def solution(mesh):
    return jax.shard_map(
        shards,
        mesh=mesh,
        in_specs=(
            P(("row", "col"), None, None),
            P(None, "row", "col"),
            P("row", None),
            P(),
            P(),
            P(),
        ),
        out_specs=P("row", "col"),
        check_vma=False,
    )
```

```python
import functools

import jax
import jax.numpy as jnp
from jax import lax
from jax.experimental import pallas as pl
from jax.experimental.pallas import tpu as pltpu
from jax.sharding import PartitionSpec as P

MESH = pl.DeviceIdType.MESH
SIDE = 4
DEPTH = 16
REACH = 4
LAST = 3
GATE = 8
SOON = 6
PIECES = (640, 2560)
PARTS = (640, 1024, 1024, 512)
POINTS = (0, 1, 2, 4)


def gather_kernel(
    amp_hbm, int_hbm, occ_hbm, eocc_hbm, evir_hbm, off_ref, out_ref,
    shard, rows, slabs, amps, both, pair, vir, stage,
    amp_ref, occ_ref, eocc_ref, evir_ref,
    local, send, near, onto, far, over, line_send, line_got, side, ready, awake,
):
    row, z = lax.axis_index("row"), lax.axis_index("col")
    x, y, core = row // 8, (row // 2) % SIDE, row % 2
    way = 1 - 2 * core
    half = int_hbm.shape[2] // 2
    mine = pl.multiple_of(core * half, 128)
    pairs = out_ref.shape[0]
    panels = (0, 1)

    def turn(v):
        return (v + SIDE) % SIDE

    def beside(axis, step, cc):
        if axis == 0:
            return {"row": (turn(x + step) * SIDE + y) * 2 + cc, "col": z}
        return {"row": (x * SIDE + turn(y + step)) * 2 + cc, "col": z}

    sibling = {"row": row + way, "col": z}

    zero = DEPTH - 1
    blocks = -(-zero // REACH)

    def down_blocks(v):
        return jnp.where(v + 2 * REACH <= zero, 2, 1)

    def blocks_at(v):
        return jnp.where(core == 0, blocks - down_blocks(v), down_blocks(v))

    def on_line(d):
        return {"row": row, "col": (z + d + DEPTH) % DEPTH}

    def gated(v, d):
        first = jnp.logical_and(v == 0, row == 0)
        up = jnp.logical_and(jnp.logical_and(v >= 0, v < GATE), jnp.logical_and(v + d <= zero, jnp.logical_not(first)))
        return jnp.where(core == 0, up, jnp.logical_and(v < d, v >= 0))

    def gated_to(d):
        return gated(z, d)

    def gated_from(d):
        return gated(jnp.where(core == 0, z - d, (z + d) % DEPTH), d)

    def sends_block(s):
        inside = jnp.logical_or(core == 0, z >= REACH)
        return jnp.logical_and(inside, blocks_at((z + way * REACH + DEPTH) % DEPTH) > s)

    def gets_block(s):
        return blocks_at(z) > s

    after = z >= GATE
    relays = jnp.logical_and(core == 0, sends_block(2))

    def fetch(i, src, dst):
        return pltpu.make_async_copy(src, dst, local.at[i])

    fetches = [
        fetch(0, int_hbm, shard),
        fetch(1, amp_hbm, amp_ref),
        fetch(2, occ_hbm, occ_ref),
        fetch(3, eocc_hbm, eocc_ref),
        fetch(4, evir_hbm, evir_ref),
    ]
    for one in fetches:
        one.start()

    barrier = pltpu.get_barrier_semaphore()

    def greet(to):
        pl.semaphore_signal(barrier, inc=1, device_id=to, device_id_type=MESH)

    latest = jnp.logical_and(row == 0, z == 0)

    def is_latest(to):
        return jnp.logical_and(to["row"] == 0, z == 0)

    by_side = is_latest(sibling)
    next_to = functools.reduce(jnp.logical_or, [is_latest(beside(axis, step, 0)) for axis in (0, 1) for step in (1, -1)])
    greeted = 9 - jnp.logical_or(by_side, next_to).astype(jnp.int32)
    around = [sibling] + [beside(axis, step, cc) for axis in (0, 1) for step in (1, -1) for cc in (0, 1)]

    @pl.when(jnp.logical_not(latest))
    def _():
        for to in around:
            greet(to)

    for d in range(1, REACH + 1):
        pl.when(gated_to(d))(functools.partial(greet, on_line(way * d)))
        pl.when(jnp.logical_not(gated_from(d)))(functools.partial(greet, on_line(-way * d)))
        greeted = greeted + gated_from(d).astype(jnp.int32) + 1 - gated_to(d).astype(jnp.int32)
    pl.semaphore_wait(barrier, greeted)

    def tell(to):
        pl.semaphore_signal(ready, inc=1, device_id=to, device_id_type=MESH)

    for d in range(1, REACH + 1):
        pl.when(gated_from(d))(functools.partial(tell, on_line(-way * d)))

    @pl.when(latest)
    def _():
        for to in around:
            pl.semaphore_signal(awake, inc=1, device_id=to, device_id_type=MESH)

    def remote(src, dst, sent, got, to):
        return pltpu.make_async_remote_copy(
            src_ref=src, dst_ref=dst, send_sem=sent, recv_sem=got, device_id=to, device_id_type=MESH
        )

    starts = [sum(PIECES[:a]) for a in range(len(PIECES))]
    begins = [sum(PARTS[:k]) for k in range(len(PARTS))]

    def place(p, along_first, along_second, cols):
        if p == 0:
            return rows.at[0, along_first, along_second, :, :, cols]
        return rows.at[1, along_second, along_first, :, :, cols]

    def own_direct(axis, step, cc):
        src = shard.at[:, :, pl.ds(pl.multiple_of(cc * half, 128), PIECES[0])]
        back = (-step) % SIDE
        spot = (slice(None), back, 0) if axis == 0 else (slice(None), 0, back)
        dst = rows.at[(*spot, core, slice(None), pl.ds(0, PIECES[0]))]
        return remote(src, dst, send.at[0], near.at[0, axis, 0, (1 - step) // 2], beside(axis, step, cc))

    def own_direct_arrived(axis, index):
        block = rows.at[:, 0, 0, :, :, pl.ds(0, PIECES[0])]
        remote(block, block, send.at[0], near.at[0, axis, 0, index], sibling).wait_recv()

    def own(a, p, phase, step):
        cols = pl.ds(starts[a], PIECES[a])
        back = (-step) % SIDE
        dst = place(p, back, 0, cols) if phase == 0 else place(p, 0, back, cols)
        axis = phase if p == 0 else 1 - phase
        return remote(place(p, 0, 0, cols), dst, send.at[0], near.at[a, p, phase, (1 - step) // 2], beside(axis, step, core))

    def own_arrived(a, p, phase, index):
        block = place(p, 0, 0, pl.ds(starts[a], PIECES[a]))
        remote(block, block, send.at[0], near.at[a, p, phase, index], sibling).wait_recv()

    def onward(a, p):
        cols = pl.ds(starts[a], PIECES[a])
        return remote(place(p, turn(-way), 0, cols), place(p, 2, 0, cols), send.at[0], onto.at[a, p], beside(p, way, core))

    def others(k, p, step):
        cols = pl.ds(begins[k], PARTS[k])
        three = pl.ds(1, SIDE - 1)
        return remote(
            place(p, three, 0, cols), place(p, three, (-step) % SIDE, cols),
            send.at[0], far.at[k, p, (1 - step) // 2], beside(1 - p, step, core),
        )

    def others_arrived(k, p, index):
        block = place(p, pl.ds(1, SIDE - 1), 0, pl.ds(begins[k], PARTS[k]))
        remote(block, block, send.at[0], far.at[k, p, index], sibling).wait_recv()

    def line_onward(k, p):
        cols = pl.ds(begins[k], PARTS[k])
        whole = pl.ds(0, SIDE)
        return remote(place(p, whole, turn(-way), cols), place(p, whole, 2, cols), send.at[0], over.at[k, p], beside(1 - p, way, core))

    def slab_block(s):
        low = zero - REACH * s if s > 0 else zero
        return slabs.at[pl.ds(low + core * (2 * (zero - low) - REACH + 1), REACH)]

    def slab_copy(d):
        return remote(slabs.at[zero], slabs.at[zero - way * d], line_send.at[d - 1], line_got.at[d - 1], on_line(way * d))

    def block_copy(s):
        i = REACH + s - 1
        return remote(slab_block(s), slab_block(s + 1), line_send.at[i], line_got.at[i], on_line(way * REACH))

    def send_gated():
        late = sum(gated_to(d).astype(jnp.int32) for d in range(1, REACH + 1))
        pl.when(late > 0)(functools.partial(pl.semaphore_wait, ready, late))
        for d in range(1, REACH + 1):
            pl.when(gated_to(d))(slab_copy(d).start)

    def line_step(s):
        if s == 0:
            own_slab.wait_recv()
            for d in range(1, REACH + 1):
                pl.when(jnp.logical_not(gated_to(d)))(slab_copy(d).start)
            pl.when(core == 0)(send_gated)
        if s == 1:
            for d in range(1, REACH + 1):
                pl.when(jnp.logical_or(core == 0, z + d <= zero))(slab_copy(d).wait_recv)
            pl.when(sends_block(1))(block_copy(1).start)
        if s == 2:
            pl.when(core == 1)(send_gated)
            pl.when(relays)(block_copy(1).wait_recv)
            pl.when(sends_block(2))(block_copy(2).start)
        if s == LAST:
            pl.when(jnp.logical_and(gets_block(1), jnp.logical_not(relays)))(block_copy(1).wait_recv)
            pl.when(gets_block(2))(block_copy(2).wait_recv)
            for d in range(1, REACH + 1):
                pl.when(jnp.logical_and(core == 1, z + d > zero))(slab_copy(d).wait_recv)
            share.start()

    halves = remote(
        shard.at[:, :, pl.ds(pl.multiple_of((1 - core) * half, 128), half)],
        rows.at[:, 0, 0, core], send.at[1], side.at[0], sibling,
    )
    own_slab = remote(slabs.at[zero, core], slabs.at[zero, core], send.at[2], side.at[1], sibling)
    pair_copy = remote(pair.at[core], pair.at[core], send.at[3], side.at[2], sibling)
    reach = REACH * LAST
    side_slabs = slabs.at[pl.ds(zero - reach + core * (reach + 1), reach)]
    share = remote(side_slabs, side_slabs, send.at[4], side.at[3], sibling)

    def result(k):
        block = out_ref.at[:, pl.ds(pl.multiple_of(mine + begins[k], 128), PARTS[k])]
        return remote(stage.at[:, pl.ds(begins[k], PARTS[k])], block, send.at[5], side.at[4], sibling)

    def denominators():
        for one in fetches[2:]:
            one.wait()
        occ_count = eocc_ref.shape[0]
        levels = jnp.broadcast_to(eocc_ref[...].reshape(1, occ_count), (pairs, occ_count)).T
        spots = lax.broadcasted_iota(jnp.int32, levels.shape, 0)
        energy = [jnp.sum(jnp.where(spots == occ_ref[i : i + 1, :], levels, 0.0), axis=0, keepdims=True) for i in (0, 1)]
        pair[core] = jnp.broadcast_to(energy[0] + energy[1], (pairs, pairs)).T
        pair_copy.start()
        virtual = evir_ref[...].reshape(1, evir_ref.shape[0])
        spots = lax.broadcasted_iota(jnp.int32, virtual.shape, 1)
        count = half // virtual.shape[1]
        lead = off_ref[0] + (2 * z + core) * count
        vir[...] = jnp.concatenate(
            [jnp.sum(jnp.where(spots == lead + a, virtual, 0.0), axis=1, keepdims=True) + virtual for a in range(count)],
            axis=1,
        )

    def split_amps():
        share.wait_recv()
        pair_copy.wait_recv()
        for a in range(DEPTH):
            ahead = (a - z + DEPTH) % DEPTH
            amps[a] = slabs[jnp.where(ahead <= REACH * down_blocks(z), zero + ahead, ahead - 1)]
        for i, c in enumerate((core, 1 - core)):
            full = amps[:, c].reshape(pairs, amps.shape[3])
            high = full.astype(jnp.bfloat16)
            both[i * pairs : (i + 1) * pairs, :] = high
            both[(2 + i) * pairs : (3 + i) * pairs, :] = (full - high.astype(jnp.float32)).astype(jnp.bfloat16)

    def compute(k):
        cols = pl.ds(begins[k], PARTS[k])
        block = jnp.concatenate(
            [rows[p, turn(i - x), turn(j - y), :, :, cols].reshape(-1, PARTS[k]) for p in panels for i in range(SIDE) for j in range(SIDE)],
            axis=0,
        )
        high = block.astype(jnp.bfloat16)
        low = (block - high.astype(jnp.float32)).astype(jnp.bfloat16)
        head = jnp.dot(both[...], high, preferred_element_type=jnp.float32)
        tail = jnp.dot(both[: 2 * pairs, :], low, preferred_element_type=jnp.float32)
        ladder = head[: 2 * pairs] + (head[2 * pairs :] + tail)
        stage[:, cols] = ladder[pairs:] / (pair[1 - core][:, 0:1] - vir[:, cols])
        result(k).start()
        spot = pl.ds(pl.multiple_of(mine + begins[k], 128), PARTS[k])
        out_ref[:, spot] = ladder[:pairs] / (pair[core][:, 0:1] - vir[:, cols])

    def send_others(k):
        for p in panels:
            for step in (1, -1):
                others(k, p, step).start()

    def send_line_onward(k):
        if k == 1:
            for p in panels:
                own_arrived(1, p, 1, core)
        for p in panels:
            others_arrived(k, p, core)
            line_onward(k, p).start()

    def finish(k):
        if k == 1:
            for p in panels:
                own_arrived(1, p, 1, 1 - core)
        for p in panels:
            others_arrived(k, p, 1 - core)
            line_onward(k, p).wait_recv()
        compute(k)

    ways = [(axis, step) for axis in (0, 1) for step in (1, -1)]

    def start_direct(held):
        for axis, step in ways:
            for cc in (0, 1):
                pl.when(is_latest(beside(axis, step, cc)) == held)(own_direct(axis, step, cc).start)

    def start_own(phase, held):
        for p in panels:
            for step in (1, -1):
                axis = phase if p == 0 else 1 - phase
                pl.when(is_latest(beside(axis, step, core)) == held)(own(1, p, phase, step).start)

    fetches[0].wait()
    start_direct(False)
    pl.when(jnp.logical_not(by_side))(halves.start)
    keep = pltpu.make_async_copy(shard.at[:, :, pl.ds(mine, half)], rows.at[:, 0, 0, core], local.at[0])
    keep.start()
    fetches[1].wait()
    width = amp_ref.shape[2]
    for p in panels:
        slabs[zero, core, :, p * width : (p + 1) * width] = amp_ref[:, p, :]
    pl.when(jnp.logical_not(by_side))(own_slab.start)

    @pl.when(by_side)
    def _():
        pl.semaphore_wait(awake, 1)
        halves.start()
        own_slab.start()

    keep.wait()
    halves.wait_recv()
    start_own(0, False)
    pl.when(after)(functools.partial(line_step, 0))

    @pl.when(next_to)
    def _():
        start_own(1, False)
        pl.semaphore_wait(awake, 1)
        start_direct(True)
        start_own(0, True)
        start_own(1, True)

    for axis in (0, 1):
        own_direct_arrived(axis, core)
    for p in panels:
        onward(0, p).start()

    @pl.when(jnp.logical_not(next_to))
    def _():
        for p in panels:
            for step in (1, -1):
                own(1, p, 1, step).start()

    def line_point(point):
        for s in range(2, LAST + 1):
            if POINTS[s] == point:
                line_step(s)

    pl.when(jnp.logical_not(after))(functools.partial(line_step, 0))
    denominators()
    for axis in (0, 1):
        own_direct_arrived(axis, 1 - core)
    for p in panels:
        onward(0, p).wait_recv()
    send_others(0)
    for p in panels:
        own_arrived(1, p, 0, core)
        onward(1, p).start()
    pl.when(z >= SOON)(functools.partial(line_step, 1))
    send_line_onward(0)
    pl.when(z < SOON)(functools.partial(line_step, 1))
    for p in panels:
        own_arrived(1, p, 0, 1 - core)
        onward(1, p).wait_recv()
    send_others(1)
    line_point(2)
    count = len(PARTS)
    finished = 0
    send_others(2)
    for k in range(1, count):
        send_line_onward(k)
        if k + 2 < count:
            send_others(k + 2)
        line_point(k + 2)
        if k + 2 == POINTS[LAST]:
            split_amps()
        if k + 2 >= POINTS[LAST]:
            while finished <= k - 2:
                finish(finished)
                finished += 1
    while finished < count:
        finish(finished)
        finished += 1

    for block in (rows.at[:, :, 0:3], rows.at[0, 0:3, 0:2]):
        remote(block, block, send.at[0], side.at[0], sibling).wait_send()
    for one in (halves, own_slab, pair_copy, share):
        one.wait_send()
    for d in range(1, REACH + 1):
        slab_copy(d).wait_send()
    for s in range(1, LAST):
        pl.when(sends_block(s))(block_copy(s).wait_send)
    all_results = remote(stage, out_ref.at[:, pl.ds(mine, half)], send.at[5], side.at[4], sibling)
    all_results.wait_send()
    all_results.wait_recv()


def store_kernel(src_ref, dst_ref, sems):
    count = sems.shape[0]
    height = src_ref.shape[0] // count
    copies = [
        pltpu.make_async_copy(src_ref.at[pl.ds(i * height, height)], dst_ref.at[pl.ds(i * height, height)], sems.at[i])
        for i in range(count)
    ]
    for one in copies:
        one.start()
    for one in copies:
        one.wait()


def gather_and_contract(amplitudes, integrals, occ_pairs, eps_occ, eps_vir, vir_offset, cid=0, name="gather_and_contract"):
    panels, depth, ab = integrals.shape
    mine, _, panel = amplitudes.shape
    pairs = occ_pairs.shape[0]
    cd = panels * panel
    half = ab // 2
    hbm = pl.BlockSpec(memory_space=pltpu.HBM)
    arrays = (amplitudes, integrals, occ_pairs.T, eps_occ, eps_vir)
    return pl.pallas_call(
        gather_kernel,
        out_shape=pltpu.VMEM((pairs, ab), jnp.float32),
        in_specs=[hbm] * 5 + [pl.BlockSpec(memory_space=pltpu.SMEM)],
        out_specs=pl.BlockSpec(memory_space=pltpu.VMEM),
        scratch_shapes=[
            pltpu.VMEM(integrals.shape, jnp.float32),
            pltpu.VMEM((panels, SIDE, SIDE, 2, depth, half), jnp.float32),
            pltpu.VMEM((2 * DEPTH - 1, 2, mine, cd), jnp.float32),
            pltpu.VMEM((DEPTH, 2, mine, cd), jnp.float32),
            pltpu.VMEM((4 * pairs, cd), jnp.bfloat16),
            pltpu.VMEM((2, pairs, pairs), jnp.float32),
            pltpu.VMEM((1, half), jnp.float32),
            pltpu.VMEM((pairs, half), jnp.float32),
            pltpu.VMEM(amplitudes.shape, jnp.float32),
            pltpu.VMEM((2, pairs), jnp.int32),
            pltpu.VMEM(eps_occ.shape, jnp.float32),
            pltpu.VMEM(eps_vir.shape, jnp.float32),
            pltpu.SemaphoreType.DMA((5,)),
            pltpu.SemaphoreType.DMA((6,)),
            pltpu.SemaphoreType.DMA((len(PIECES), 2, 2, 2)),
            pltpu.SemaphoreType.DMA((len(PIECES), 2)),
            pltpu.SemaphoreType.DMA((len(PARTS), 2, 2)),
            pltpu.SemaphoreType.DMA((len(PARTS), 2)),
            pltpu.SemaphoreType.DMA((REACH + LAST - 1,)),
            pltpu.SemaphoreType.DMA((REACH + LAST - 1,)),
            pltpu.SemaphoreType.DMA((5,)),
            pltpu.SemaphoreType.REGULAR,
            pltpu.SemaphoreType.REGULAR,
        ],
        compiler_params=pltpu.CompilerParams(
            collective_id=cid, has_side_effects=True, vmem_limit_bytes=40 * 1024 * 1024
        ),
        cost_estimate=pl.CostEstimate(
            flops=2 * pairs * cd * ab * 3, bytes_accessed=4 * (pairs * ab + panels * depth * ab), transcendentals=0
        ),
        name=name,
    )(*(pltpu.with_memory_space_constraint(a, pltpu.HBM) for a in arrays), vir_offset)


def shards(amplitudes, integrals, occ_pairs, eps_occ, eps_vir, vir_offset):
    update = gather_and_contract(amplitudes, integrals, occ_pairs, eps_occ, eps_vir, vir_offset)
    return pl.pallas_call(
        store_kernel,
        out_shape=jax.ShapeDtypeStruct(update.shape, jnp.float32),
        in_specs=[pl.BlockSpec(memory_space=pltpu.VMEM)],
        out_specs=pl.BlockSpec(memory_space=pl.ANY),
        scratch_shapes=[pltpu.SemaphoreType.DMA((8,))],
        cost_estimate=pl.CostEstimate(flops=0, bytes_accessed=4 * update.size, transcendentals=0),
        name="store",
    )(pltpu.with_memory_space_constraint(update, pltpu.VMEM))


def solution(mesh):
    return jax.shard_map(
        shards,
        mesh=mesh,
        in_specs=(
            P(("row", "col"), None, None),
            P(None, "row", "col"),
            P("row", None),
            P(),
            P(),
            P(),
        ),
        out_specs=P("row", "col"),
        check_vma=False,
    )
```
